256 devices in a mesh: seq: 64 (over y, z, core), kvh: 4 (over x).
Axes of the slice: x: 4, y: 4, z: 8, core: 2. Of those that a mesh axis runs over, the one named last changes fastest.
Arguments:
- queries: bfloat16 [128, 64, 128], P('seq', 'kvh')
- cache_keys: bfloat16 [131072, 8, 128], P('seq', 'kvh'), may hold values from -6 to 6
- cache_values: bfloat16 [131072, 8, 128], P('seq', 'kvh'), may hold values from -6 to 6
- new_keys: bfloat16 [128, 8, 128], P('seq', 'kvh'), may hold values from -6 to 6
- new_values: bfloat16 [128, 8, 128], P('seq', 'kvh'), may hold values from -6 to 6
- doc_start: int32 [128, 2], replicated, may hold values from 0 to 255, as said below
- doc_count: int32 [128, 2], replicated, may hold values from 1 to 64
Outputs:
- attended: bfloat16 [128, 64, 128], P('seq', 'kvh')
The draws below stay inside these ranges and needn't reach their ends.
Inputs may be any that keep to these rules, and one draw needn't show every extreme that they name: doc_start[r, i] + doc_count[r, i] <= 256.
All inputs are finite; a program needn't handle non-finite values.
Results may differ from the reference program's by a relative error of at most 0.0048.
Values may be sent and summed in bfloat16 or wider, within the bound.
A program may use at most 256 MiB of HBM per device.

```python
import jax
import jax.numpy as jnp
from jax import lax

QH = 64
KVH = 8
HD = 128
ROWS = 128
BLOCK = 512
DOCS = 2
TOK_DEV = 2048
TOKENS = 131072
BLK_DEV = 4
NBLK = 256
MAXB = 64
N_SEQ = 64


def documents(key):
    count_key, start_key = jax.random.split(jax.random.fold_in(key, 71))
    count = jax.random.randint(count_key, (ROWS, DOCS), 1, MAXB + 1)
    count = count.at[0, 0].set(MAXB).at[1, 0].set(1)
    offset = jax.random.randint(start_key, (ROWS, DOCS), 0, 1 << 20)
    start = offset % (NBLK - count + 1)
    start = start.at[1, 0].set(NBLK - 1).at[2, 0].set(0)
    return (start.astype(jnp.int32), count.astype(jnp.int32))


def draw_doc_start(key, part):
    return documents(key)[0]


def draw_doc_count(key, part):
    return documents(key)[1]


def draw_queries(key, part):
    key = jax.random.fold_in(key, 5)
    base = jax.random.normal(key, (ROWS, QH, HD), jnp.float32)
    return base.astype(jnp.bfloat16)


def steps_of(rng, shape, cuts, smallest, high):
    factor_of, own = 1.0, jax.random.fold_in(rng, 6)
    for dim, parts in cuts:
        heights = jnp.exp(jax.random.uniform(jax.random.fold_in(own, dim), (parts,), jnp.float32, smallest / len(cuts), high / len(cuts)))
        factor_of = factor_of * jnp.repeat(heights, shape[dim] // parts).reshape([-1 if axis == dim else 1 for axis in range(len(shape))])
    return factor_of


def noise(stream_key, shape, deviation, most, shards=(), held_as=jnp.bfloat16):
    entries = jax.random.normal(stream_key, shape, jnp.float32) * deviation
    if len(shards) > 0:
        entries = steps_of(stream_key, shape, shards, -0.22, 0.18) * entries
    return jnp.clip(entries, min=-most, max=most).astype(held_as)


def setup_inputs(seed: int = 0) -> dict:
    streams_of = jax.random.split(jax.random.key(seed), 8)
    queries = draw_queries(jax.random.fold_in(streams_of[7], 71), 0)
    cache_keys = noise(streams_of[1], (TOKENS, KVH, HD), 1.0, 6.0, ((0, 64), (1, 4)))
    cache_values = noise(streams_of[2], (TOKENS, KVH, HD), 1.0, 6.0, ((0, 64), (1, 4)))
    new_keys = noise(streams_of[3], (ROWS, KVH, HD), 1.0, 6.0, ((0, 64), (1, 4)))
    new_values = noise(streams_of[4], (ROWS, KVH, HD), 1.0, 6.0, ((0, 64), (1, 4)))
    doc_start = draw_doc_start(jax.random.fold_in(streams_of[7], 71), 0)
    doc_count = draw_doc_count(jax.random.fold_in(streams_of[7], 71), 0)
    return {"queries": queries, "cache_keys": cache_keys, "cache_values": cache_values, "new_keys": new_keys, "new_values": new_values, "doc_start": doc_start, "doc_count": doc_count}


NEG = -1e30


def allowed_mask(doc_start, doc_count, segment):
    blocks = segment * BLK_DEV + jnp.arange(BLK_DEV, dtype=jnp.int32)
    inside = (doc_start[:, :, None] <= blocks[None, None, :]) & (blocks[None, None, :] < (doc_start + doc_count)[:, :, None])
    return jnp.repeat(jnp.any(inside, axis=1), BLOCK, axis=1)


def reference(queries, cache_keys, cache_values, new_keys, new_values, doc_start, doc_count):
    group = QH // KVH
    scale = HD ** -0.5
    q_four = queries.reshape(ROWS, KVH, group, HD).astype(jnp.float32)
    keys = cache_keys.reshape(N_SEQ, TOK_DEV, KVH, HD)
    values = cache_values.reshape(N_SEQ, TOK_DEV, KVH, HD)

    def segment_state(items):
        key_seg, value_seg, segment = items
        mask = allowed_mask(doc_start, doc_count, segment)[None, None]
        scores = jnp.einsum("rgjd,tgd->gjrt", q_four, key_seg.astype(jnp.float32)) * scale
        top = jnp.max(jnp.where(mask, scores, NEG), axis=-1)
        probs = jnp.where(mask, jnp.exp(scores - top[..., None]), 0.0)
        total = jnp.sum(probs, axis=-1)
        rounded = probs.astype(jnp.bfloat16).astype(jnp.float32)
        out = jnp.einsum("gjrt,tgd->gjrd", rounded, value_seg.astype(jnp.float32))
        return out, top, total

    outs, tops, totals = lax.map(segment_state, (keys, values, jnp.arange(N_SEQ, dtype=jnp.int32)))
    high = jnp.max(tops, axis=0)
    weight = jnp.exp(tops - high[None])
    whole = jnp.sum(outs * weight[..., None], axis=0)
    norm = jnp.sum(totals * weight, axis=0)
    own = jnp.einsum("rgjd,rgd->gjr", q_four, new_keys.astype(jnp.float32)) * scale
    high_two = jnp.maximum(high, own)
    keep = jnp.exp(high - high_two)
    fresh = jnp.exp(own - high_two)
    value_new = jnp.transpose(new_values.astype(jnp.float32), (1, 0, 2))[:, None]
    whole = whole * keep[..., None] + fresh[..., None] * value_new
    norm = norm * keep + fresh
    result = whole / norm[..., None]
    return jnp.transpose(result, (2, 0, 1, 3)).reshape(ROWS, QH, HD).astype(jnp.bfloat16)
```

```python
import functools
import math

import jax
import jax.numpy as jnp
from jax import lax
from jax.experimental import pallas as pl
from jax.experimental.pallas import tpu as pltpu
from jax.sharding import PartitionSpec as P

MESH = pl.DeviceIdType.MESH
HD = 128
BLOCK = 512
NBLOCKS = 4
TOK = BLOCK * NBLOCKS
NEG = -1e30
SCALE2 = HD ** (-0.5) * math.log2(math.e)
F32 = jnp.float32
BF16 = jnp.bfloat16


def lanes_of(rows):
    return lax.broadcasted_iota(jnp.int32, (rows, 128), 1)


def encode(stat, count):
    stat = jnp.where(lanes_of(16) < count, stat, 0.0)
    high = stat.astype(BF16).astype(F32)
    rest = stat - high
    middle = rest.astype(BF16).astype(F32)
    low = rest - middle
    return high + pltpu.roll(middle, 32, 1) + pltpu.roll(low, 64, 1)


def decode(tile):
    tile = tile.astype(F32)
    return tile + pltpu.roll(tile, 96, 1) + pltpu.roll(tile, 64, 1)


def weights_of(stats):
    top = functools.reduce(jnp.maximum, stats)
    raw = [jnp.exp2(s - top) for s in stats]
    total = functools.reduce(jnp.add, raw)
    inverse = 1.0 / total
    return [w * inverse for w in raw], top + jnp.log2(total)


def two_columns(weight, g, column):
    part = weight[g * 8 : (g + 1) * 8]
    return jnp.concatenate(
        [jnp.broadcast_to(part[:, column + r : column + r + 1], (8, 128)) for r in range(2)], axis=0
    )


def kernel(
    ny, nz,
    q_ref, k_hbm, v_hbm, nk_ref, nv_ref, start_ref, count_ref, out_ref,
    qbuf, bias, kraw, vraw, temp, kaug, vaug, scores,
    core_out, core_in, y_out, y_in, z_out, z_in,
    load_sem, qz_send, qz_recv, qy_send, qy_recv, qc_send, qc_recv,
    c_send, c_recv, y_send, y_recv, z_send, z_recv,
):
    seq = lax.axis_index("seq")
    x = lax.axis_index("kvh")
    core = lax.rem(seq, 2)
    z = lax.rem(lax.div(seq, 2), nz)
    y = lax.div(seq, 2 * nz)
    other = 1 - core

    def device(yy, zz, cc):
        return ((yy * nz + zz) * 2 + cc, x)

    loads = [
        pltpu.make_async_copy(k_hbm, kraw, load_sem.at[0]),
        pltpu.make_async_copy(v_hbm, vraw, load_sem.at[1]),
    ]
    for load in loads:
        load.start()

    barrier = pltpu.get_barrier_semaphore()
    peers = (
        [device(y, lax.rem(z + k, nz), core) for k in range(1, nz)]
        + [device(lax.rem(y + k, ny), z, core) for k in range(1, ny)]
        + [device(y, z, other)]
    )
    for peer in peers:
        pl.semaphore_signal(barrier, inc=1, device_id=peer, device_id_type=MESH)

    q_own = q_ref[...].astype(F32)
    for g in range(2):
        qbuf[core, y, z, g] = jnp.concatenate(
            [q_own[r, g * 8 : (g + 1) * 8] for r in range(2)], axis=0
        ).astype(BF16)
    pl.semaphore_wait(barrier, len(peers))

    def remote(src, dst, send, recv, peer):
        return pltpu.make_async_remote_copy(
            src_ref=src, dst_ref=dst, send_sem=send, recv_sem=recv, device_id=peer, device_id_type=MESH
        )

    def qz_copy(k):
        mine = qbuf.at[core, y, z]
        return remote(mine, mine, qz_send.at[k - 1], qz_recv.at[k - 1], device(y, lax.rem(z + k, nz), core))

    def qz_arrival(k):
        there = qbuf.at[core, y, lax.rem(z - k + nz, nz)]
        return remote(there, there, qz_send.at[k - 1], qz_recv.at[k - 1], device(y, lax.rem(z + k, nz), core))

    for k in range(1, nz):
        qz_copy(k).start()

    block = seq * NBLOCKS + lanes_of(8)

    def row_bias(row):
        seen = None
        for i in range(2):
            first = start_ref[i, row]
            inside = (block >= first) & (block < first + count_ref[i, row])
            seen = inside if seen is None else seen | inside
        return jnp.where(seen | (lanes_of(8) >= NBLOCKS), 0.0, NEG)

    def fill_bias(source, carry):
        yy = lax.div(source, 2 * nz)
        zz = lax.rem(lax.div(source, 2), nz)
        cc = lax.rem(source, 2)
        bias[cc, yy, zz] = jnp.concatenate([row_bias(2 * source), row_bias(2 * source + 1)], axis=0).astype(BF16)
        return carry

    lax.fori_loop(0, 2 * ny * nz, fill_bias, 0)

    piece = 256
    for load in loads:
        load.wait()

    def split(i, carry):
        at = pl.multiple_of(i * piece, piece)
        flat = pl.multiple_of(i * 2 * piece, 2 * piece)
        indicator = (lanes_of(piece) == lax.div(at, BLOCK)).astype(F32).astype(BF16)
        temp[0] = kraw[pl.ds(flat, 2 * piece), :].astype(F32)
        temp[1] = vraw[pl.ds(flat, 2 * piece), :].astype(F32)
        for g in range(2):
            kaug[g, pl.ds(at, piece), 0:128] = temp[0, pl.ds(g, piece, stride=2), :].astype(BF16)
            kaug[g, pl.ds(at, piece), 128:256] = indicator
            vaug[g, pl.ds(at, piece), 0:128] = temp[1, pl.ds(g, piece, stride=2), :].astype(BF16)
            vaug[g, pl.ds(at, piece), 128:256] = jnp.ones((piece, 128), BF16)
        return carry

    lax.fori_loop(0, TOK // piece, split, 0)

    for k in range(1, nz):
        qz_arrival(k).wait_recv()

    def qy_copy(k):
        mine = qbuf.at[core, y]
        return remote(mine, mine, qy_send.at[k - 1], qy_recv.at[k - 1], device(lax.rem(y + k, ny), z, core))

    def qy_arrival(k):
        there = qbuf.at[core, lax.rem(y - k + ny, ny)]
        return remote(there, there, qy_send.at[k - 1], qy_recv.at[k - 1], device(lax.rem(y + k, ny), z, core))

    def qc_copy(i):
        mine = qbuf.at[core, lax.rem(y - i + ny, ny)]
        return remote(mine, mine, qc_send.at[i], qc_recv.at[i], device(y, z, other))

    def qc_arrival(i):
        there = qbuf.at[other, lax.rem(y - i + ny, ny)]
        return remote(there, there, qc_send.at[i], qc_recv.at[i], device(y, z, other))

    for k in range(1, ny):
        qy_copy(k).start()
    qc_copy(0).start()

    rows = 16 * nz

    def c_copy(i):
        yy = lax.rem(y - i + ny, ny)
        return remote(core_out.at[0, yy], core_in.at[yy], c_send.at[i], c_recv.at[i], device(y, z, other))

    def attend(yy):
        stats = [[None] * 2, [None] * 2]
        for g in range(2):
            lhs = jnp.concatenate(
                [
                    jnp.concatenate([qbuf[cc, yy, :, g].reshape(rows, 128), bias[cc, yy].reshape(rows, 128)], axis=1)
                    for cc in (other, core)
                ],
                axis=0,
            )
            top = None
            for b in range(NBLOCKS):
                s = lax.dot_general(
                    lhs, kaug[g, b * BLOCK : (b + 1) * BLOCK, :], (((1,), (1,)), ((), ())),
                    preferred_element_type=F32,
                )
                scores[g, :, b * BLOCK : (b + 1) * BLOCK] = s
                for i in range(BLOCK // 128):
                    part = s[:, i * 128 : (i + 1) * 128]
                    top = part if top is None else jnp.maximum(top, part)
            top = jnp.max(top, axis=1, keepdims=True)
            total = jnp.zeros((2 * rows, 256), F32)
            for b in range(NBLOCKS):
                s = scores[g, :, b * BLOCK : (b + 1) * BLOCK]
                p = jnp.exp2((s - top) * SCALE2).astype(BF16)
                total = total + jnp.dot(p, vaug[g, b * BLOCK : (b + 1) * BLOCK, :], preferred_element_type=F32)
            norm = total[:, 128:256]
            out = total[:, 0:128] * (1.0 / norm)
            stat = top * SCALE2 + jnp.log2(norm)
            for part in range(2):
                packed = jnp.zeros((8, 128), F32)
                for k in range(2 * nz):
                    at = part * rows + k * 8
                    packed = jnp.where(lanes_of(8) == k, stat[at : at + 8], packed)
                stats[part][g] = packed
                for zz in range(nz):
                    at = part * rows + zz * 16
                    core_out[part, yy, zz * 2 + g] = out[at : at + 16].astype(BF16)
        for part in range(2):
            core_out[part, yy, 2 * nz] = encode(jnp.concatenate(stats[part], axis=0), 2 * nz).astype(BF16)

    def merge(parts, put, put_stat):
        weights, stat = weights_of([decode(part[2 * nz]) for part in parts])
        for zz in range(nz):
            for g in range(2):
                tile = None
                for part, weight in zip(parts, weights):
                    term = part[zz * 2 + g].astype(F32) * two_columns(weight, g, 2 * zz)
                    tile = term if tile is None else tile + term
                put(zz, g, tile.astype(BF16))
        put_stat(encode(stat, 2 * nz))

    def y_copy(i):
        yy = lax.rem(y - i + ny, ny)
        return remote(y_out.at[yy], y_in.at[i - 1], y_send.at[i - 1], y_recv.at[i - 1], device(yy, z, core))

    def merge_cores(i):
        yy = lax.rem(y - i + ny, ny)
        c_copy(i).wait_recv()

        def put(zz, g, tile):
            y_out[yy, zz * 2 + g] = tile

        def put_stat(tile):
            y_out[yy, 2 * nz] = tile.astype(BF16)

        merge([core_out.at[1, yy], core_in.at[yy]], put, put_stat)

    def step(i, carry):
        @pl.when(i == 1)
        def _():
            for k in range(1, ny):
                qy_arrival(k).wait_recv()
                qc_copy(k).start()

        qc_arrival(i).wait_recv()
        attend(lax.rem(y - i + ny, ny))
        c_copy(i).start()

        @pl.when(i >= 1)
        def _():
            merge_cores(i - 1)

            @pl.when(i >= 2)
            def _():
                y_copy(i - 1).start()

        return carry

    lax.fori_loop(0, ny, step, 0)
    merge_cores(ny - 1)
    y_copy(ny - 1).start()

    for i in range(1, ny):
        y_copy(i).wait_recv()

    def put_z(zz, g, tile):
        z_out[zz, g] = tile

    def put_z_stat(tile):
        for zz in range(nz):
            z_out[zz, 2] = (tile if zz == 0 else pltpu.roll(tile, 128 - 2 * zz, 1)).astype(BF16)

    merge([y_out.at[y]] + [y_in.at[i] for i in range(ny - 1)], put_z, put_z_stat)

    def z_copy(k):
        zz = lax.rem(z + k, nz)
        return remote(z_out.at[zz], z_in.at[k - 1], z_send.at[k - 1], z_recv.at[k - 1], device(y, zz, core))

    for k in range(1, nz):
        z_copy(k).start()

    own = [None, None]
    for g in range(2):
        packed = jnp.zeros((8, 128), F32)
        for r in range(2):
            key = nk_ref[r].astype(F32)[g : g + 1]
            dots = jnp.sum(q_own[r, g * 8 : (g + 1) * 8] * key, axis=1, keepdims=True) * SCALE2
            packed = jnp.where(lanes_of(8) == r, dots, packed)
        own[g] = packed
    own = jnp.concatenate(own, axis=0)

    for k in range(1, nz):
        z_copy(k).wait_recv()

    parts = [z_out.at[z]] + [z_in.at[k] for k in range(nz - 1)]
    weights, _ = weights_of([decode(part[2]) for part in parts] + [own])
    tiles = []
    for g in range(2):
        tile = None
        for part, weight in zip(parts, weights):
            term = part[g].astype(F32) * two_columns(weight, g, 0)
            tile = term if tile is None else tile + term
        value = jnp.concatenate(
            [jnp.broadcast_to(nv_ref[r].astype(F32)[g : g + 1], (8, 128)) for r in range(2)], axis=0
        )
        tiles.append(tile + value * two_columns(weights[-1], g, 0))
    for r in range(2):
        out_ref[r] = jnp.concatenate([tiles[g][r * 8 : (r + 1) * 8] for g in range(2)], axis=0).astype(BF16)

    for k in range(1, nz):
        qz_copy(k).wait_send()
        z_copy(k).wait_send()
    for k in range(1, ny):
        qy_copy(k).wait_send()
        y_copy(k).wait_send()
    for i in range(ny):
        qc_copy(i).wait_send()
        c_copy(i).wait_send()


def per_device(ny, nz, queries, cache_keys, cache_values, new_keys, new_values, doc_start, doc_count):
    vmem = pl.BlockSpec(memory_space=pltpu.VMEM)
    smem = pl.BlockSpec(memory_space=pltpu.SMEM)
    hbm = pl.BlockSpec(memory_space=pl.ANY)
    dma = pltpu.SemaphoreType.DMA
    block = 2 * nz + 1
    return pl.pallas_call(
        functools.partial(kernel, ny, nz),
        out_shape=jax.ShapeDtypeStruct(queries.shape, BF16),
        in_specs=[vmem, hbm, hbm, vmem, vmem, smem, smem],
        out_specs=vmem,
        scratch_shapes=[
            pltpu.VMEM((2, ny, nz, 2, 16, 128), BF16),
            pltpu.VMEM((2, ny, nz, 16, 128), BF16),
            pltpu.VMEM((2 * TOK, 128), BF16),
            pltpu.VMEM((2 * TOK, 128), BF16),
            pltpu.VMEM((2, 512, 128), F32),
            pltpu.VMEM((2, TOK, 256), BF16),
            pltpu.VMEM((2, TOK, 256), BF16),
            pltpu.VMEM((2, 32 * nz, TOK), F32),
            pltpu.VMEM((2, ny, block, 16, 128), BF16),
            pltpu.VMEM((ny, block, 16, 128), BF16),
            pltpu.VMEM((ny, block, 16, 128), BF16),
            pltpu.VMEM((ny - 1, block, 16, 128), BF16),
            pltpu.VMEM((nz, 3, 16, 128), BF16),
            pltpu.VMEM((nz - 1, 3, 16, 128), BF16),
            dma((2,)),
            dma((nz - 1,)), dma((nz - 1,)),
            dma((ny - 1,)), dma((ny - 1,)),
            dma((ny,)), dma((ny,)),
            dma((ny,)), dma((ny,)),
            dma((ny - 1,)), dma((ny - 1,)),
            dma((nz - 1,)), dma((nz - 1,)),
        ],
        compiler_params=pltpu.CompilerParams(
            collective_id=0, has_side_effects=True, vmem_limit_bytes=60 * 1024 * 1024
        ),
        name="attention",
    )(
        queries,
        cache_keys.reshape(2 * TOK, 128),
        cache_values.reshape(2 * TOK, 128),
        new_keys,
        new_values,
        doc_start.T,
        doc_count.T,
    )


def solution(mesh):
    ny, nz = 4, mesh.shape["seq"] // 8
    placed = (P("seq", "kvh", None),) * 5 + (P(), P())
    return jax.shard_map(
        functools.partial(per_device, ny, nz),
        mesh=mesh,
        in_specs=placed,
        out_specs=P("seq", "kvh", None),
        check_vma=False,
    )
```

```python
import functools
import math

import jax
import jax.numpy as jnp
from jax import lax
from jax.experimental import pallas as pl
from jax.experimental.pallas import tpu as pltpu
from jax.sharding import PartitionSpec as P

MESH = pl.DeviceIdType.MESH
HD = 128
BLOCK = 512
NBLOCKS = 4
TOK = BLOCK * NBLOCKS
NEG = -1e30
SCALE2 = HD ** (-0.5) * math.log2(math.e)
F32 = jnp.float32
BF16 = jnp.bfloat16


def lanes_of(rows):
    return lax.broadcasted_iota(jnp.int32, (rows, 128), 1)


def encode(stat, count):
    stat = jnp.where(lanes_of(16) < count, stat, 0.0)
    high = stat.astype(BF16).astype(F32)
    rest = stat - high
    middle = rest.astype(BF16).astype(F32)
    low = rest - middle
    return high + pltpu.roll(middle, 32, 1) + pltpu.roll(low, 64, 1)


def decode(tile):
    tile = tile.astype(F32)
    return tile + pltpu.roll(tile, 96, 1) + pltpu.roll(tile, 64, 1)


def weights_of(stats):
    top = functools.reduce(jnp.maximum, stats)
    raw = [jnp.exp2(s - top) for s in stats]
    total = functools.reduce(jnp.add, raw)
    inverse = 1.0 / total
    return [w * inverse for w in raw], top + jnp.log2(total)


def two_columns(weight, g, column):
    part = weight[g * 8 : (g + 1) * 8]
    return jnp.concatenate(
        [jnp.broadcast_to(part[:, column + r : column + r + 1], (8, 128)) for r in range(2)], axis=0
    )


def by_distance(n):
    return sorted(range(1, n), key=lambda k: -min(k, n - k))


def kernel(
    ny, nz,
    q_hbm, k_hbm, v_hbm, nk_hbm, nv_hbm, start_hbm, count_hbm, out_ref,
    q_ref, nk_ref, nv_ref, start_ref, count_ref,
    qbuf, bias, kraw, vraw, temp, kaug, vaug, scores,
    y_out, y_in, z_out, z_in,
    load_sem, kv_send, kv_recv, qz_send, qz_recv, qy_send, qy_recv,
    y_send, y_recv, z_send, z_recv,
):
    half = nz // 2
    seq = lax.axis_index("seq")
    x = lax.axis_index("kvh")
    core = lax.rem(seq, 2)
    z = lax.rem(lax.div(seq, 2), nz)
    y = lax.div(seq, 2 * nz)
    other = 1 - core

    def device(yy, zz, cc):
        return ((yy * nz + zz) * 2 + cc, x)

    def remote(src, dst, send, recv, peer):
        return pltpu.make_async_remote_copy(
            src_ref=src, dst_ref=dst, send_sem=send, recv_sem=recv, device_id=peer, device_id_type=MESH
        )

    loads = [
        pltpu.make_async_copy(src, dst, load_sem.at[i])
        for i, (src, dst) in enumerate(
            [
                (q_hbm, q_ref), (start_hbm, start_ref), (count_hbm, count_ref),
                (k_hbm, kraw.at[0]), (v_hbm, vraw.at[0]), (nk_hbm, nk_ref), (nv_hbm, nv_ref),
            ]
        )
    ]
    for load in loads:
        load.start()

    barrier = pltpu.get_barrier_semaphore()
    peers = sorted(
        [(-min(k, nz - k), 0, k) for k in range(1, nz)] + [(-min(k, ny - k), 1, k) for k in range(1, ny)]
    )
    for _, axis, k in peers:
        peer = device(lax.rem(y + k, ny), z, core) if axis else device(y, lax.rem(z + k, nz), core)
        pl.semaphore_signal(barrier, inc=1, device_id=peer, device_id_type=MESH)
    pl.semaphore_signal(barrier, inc=1, device_id=device(y, z, other), device_id_type=MESH)

    loads[0].wait()
    q_own = q_ref[...].astype(F32)
    for g in range(2):
        qbuf[y, z, g] = jnp.concatenate([q_own[r, g * 8 : (g + 1) * 8] for r in range(2)], axis=0).astype(BF16)
    pl.semaphore_wait(barrier, len(peers) + 1)

    def qz_copy(k):
        mine = qbuf.at[y, z]
        return remote(mine, mine, qz_send.at[k - 1], qz_recv.at[z], device(y, lax.rem(z + k, nz), core))

    for k in by_distance(nz):
        qz_copy(k).start()
    swaps = [
        remote(src, dst, kv_send.at[i], kv_recv.at[i], device(y, z, other))
        for i, (src, dst) in enumerate([(k_hbm, kraw.at[1]), (v_hbm, vraw.at[1])])
    ]
    for swap in swaps:
        swap.start()

    lane = lanes_of(8)
    block = jnp.where(lane < NBLOCKS, seq * NBLOCKS + lane, (seq + 1 - 2 * core) * NBLOCKS + lane - NBLOCKS)

    def row_bias(row):
        seen = None
        for i in range(2):
            first = start_ref[i, row]
            inside = (block >= first) & (block < first + count_ref[i, row])
            seen = inside if seen is None else seen | inside
        return jnp.where(seen | (lane >= 2 * NBLOCKS), 0.0, NEG)

    def fill_bias(i, carry):
        row = 4 * i + 2 * core
        bias[lax.div(i, nz), lax.rem(i, nz)] = jnp.concatenate([row_bias(row), row_bias(row + 1)], axis=0).astype(BF16)
        return carry

    loads[1].wait()
    loads[2].wait()
    lax.fori_loop(0, ny * nz, fill_bias, 0)

    piece = 256

    def split(which):
        def body(i, carry):
            at = pl.multiple_of(which * TOK + i * piece, piece)
            flat = pl.multiple_of(i * 2 * piece, 2 * piece)
            indicator = (lanes_of(piece) == lax.div(at, BLOCK)).astype(F32).astype(BF16)
            temp[0] = kraw[which, pl.ds(flat, 2 * piece), :].astype(F32)
            temp[1] = vraw[which, pl.ds(flat, 2 * piece), :].astype(F32)
            for g in range(2):
                kaug[g, pl.ds(at, piece), 0:128] = temp[0, pl.ds(g, piece, stride=2), :].astype(BF16)
                kaug[g, pl.ds(at, piece), 128:256] = indicator
                vaug[g, pl.ds(at, piece), 0:128] = temp[1, pl.ds(g, piece, stride=2), :].astype(BF16)
                vaug[g, pl.ds(at, piece), 128:256] = jnp.ones((piece, 128), BF16)
            return carry

        lax.fori_loop(0, TOK // piece, body, 0)

    loads[3].wait()
    loads[4].wait()
    split(0)

    def qy_copy(w, k):
        mine = qbuf.at[y, pl.ds(w * half, half)]
        return remote(mine, mine, qy_send.at[w, k - 1], qy_recv.at[w, k - 1], device(lax.rem(y + k, ny), z, core))

    def qy_arrival(w, k):
        there = qbuf.at[lax.rem(y - k + ny, ny), pl.ds(w * half, half)]
        return remote(there, there, qy_send.at[w, k - 1], qy_recv.at[w, k - 1], device(lax.rem(y + k, ny), z, core))

    for w in range(2):
        for i in range(half):
            zz = w * half + i

            @pl.when(zz != z)
            def _():
                there = qbuf.at[y, zz]
                remote(there, there, qz_send.at[0], qz_recv.at[zz], device(y, zz, core)).wait_recv()

        for k in by_distance(ny):
            qy_copy(w, k).start()

    for swap in swaps:
        swap.wait_recv()
    split(1)

    rows = 16 * half

    def attend(w):
        stats = [[None] * 2 for _ in range(ny)]
        for g in range(2):
            queries = qbuf[:, pl.ds(w * half, half), g].reshape(ny * rows, 128)
            lhs = jnp.concatenate([queries, bias[:, pl.ds(w * half, half)].reshape(ny * rows, 128)], axis=1)
            top = None
            for b in range(2 * NBLOCKS):
                s = lax.dot_general(
                    lhs, kaug[g, b * BLOCK : (b + 1) * BLOCK, :], (((1,), (1,)), ((), ())),
                    preferred_element_type=F32,
                )
                scores[g, :, b * BLOCK : (b + 1) * BLOCK] = s
                for i in range(BLOCK // 128):
                    part = s[:, i * 128 : (i + 1) * 128]
                    top = part if top is None else jnp.maximum(top, part)
            top = jnp.max(top, axis=1, keepdims=True)
            total = jnp.zeros((ny * rows, 256), F32)
            for b in range(2 * NBLOCKS):
                s = scores[g, :, b * BLOCK : (b + 1) * BLOCK]
                p = jnp.exp2((s - top) * SCALE2).astype(BF16)
                total = total + jnp.dot(p, vaug[g, b * BLOCK : (b + 1) * BLOCK, :], preferred_element_type=F32)
            norm = total[:, 128:256]
            out = total[:, 0:128] * (1.0 / norm)
            stat = top * SCALE2 + jnp.log2(norm)
            for yy in range(ny):
                packed = jnp.zeros((8, 128), F32)
                for k in range(2 * half):
                    at = yy * rows + k * 8
                    packed = jnp.where(lane == k, stat[at : at + 8], packed)
                stats[yy][g] = packed
                for i in range(half):
                    at = yy * rows + i * 16
                    y_out[w, yy, i * 2 + g] = out[at : at + 16].astype(BF16)
        for yy in range(ny):
            y_out[w, yy, 2 * half] = encode(jnp.concatenate(stats[yy], axis=0), 2 * half).astype(BF16)

    def y_copy(w, k):
        yy = lax.rem(y + k, ny)
        return remote(
            y_out.at[w, yy], y_in.at[w, k - 1], y_send.at[w, k - 1], y_recv.at[w, k - 1], device(yy, z, core)
        )

    def forward(w, carry):
        for k in range(1, ny):
            qy_arrival(w, k).wait_recv()
        attend(w)
        for k in by_distance(ny):
            y_copy(w, k).start()
        return carry

    lax.fori_loop(0, 2, forward, 0)

    def z_copy(zz):
        return remote(z_out.at[zz], z_in.at[z], z_send.at[zz], z_recv.at[z], device(y, zz, core))

    def back(w, carry):
        for k in range(1, ny):
            y_copy(w, k).wait_recv()
        parts = [y_out.at[w, y]] + [y_in.at[w, k] for k in range(ny - 1)]
        weights, stat = weights_of([decode(part[2 * half]) for part in parts])
        stat = encode(stat, 2 * half)
        for i in range(half):
            for g in range(2):
                tile = None
                for part, weight in zip(parts, weights):
                    term = part[i * 2 + g].astype(F32) * two_columns(weight, g, 2 * i)
                    tile = term if tile is None else tile + term
                z_out[w * half + i, g] = tile.astype(BF16)
            z_out[w * half + i, 2] = (stat if i == 0 else pltpu.roll(stat, 128 - 2 * i, 1)).astype(BF16)
        for i in range(half):
            zz = w * half + lax.rem(z + i, half)

            @pl.when(zz != z)
            def _():
                z_copy(zz).start()

        return carry

    lax.fori_loop(0, 2, back, 0)

    loads[5].wait()
    loads[6].wait()
    z_in[z] = z_out[z]
    own = [None, None]
    for g in range(2):
        packed = jnp.zeros((8, 128), F32)
        for r in range(2):
            key = nk_ref[r].astype(F32)[g : g + 1]
            dots = jnp.sum(q_own[r, g * 8 : (g + 1) * 8] * key, axis=1, keepdims=True) * SCALE2
            packed = jnp.where(lane == r, dots, packed)
        own[g] = packed
    own = jnp.concatenate(own, axis=0)

    for k in range(1, nz):
        zz = lax.rem(z + k, nz)
        remote(z_out.at[zz], z_in.at[zz], z_send.at[zz], z_recv.at[zz], device(y, zz, core)).wait_recv()

    parts = [z_in.at[k] for k in range(nz)]
    weights, _ = weights_of([decode(part[2]) for part in parts] + [own])
    tiles = []
    for g in range(2):
        tile = None
        for part, weight in zip(parts, weights):
            term = part[g].astype(F32) * two_columns(weight, g, 0)
            tile = term if tile is None else tile + term
        value = jnp.concatenate(
            [jnp.broadcast_to(nv_ref[r].astype(F32)[g : g + 1], (8, 128)) for r in range(2)], axis=0
        )
        tiles.append(tile + value * two_columns(weights[-1], g, 0))
    for r in range(2):
        out_ref[r] = jnp.concatenate([tiles[g][r * 8 : (r + 1) * 8] for g in range(2)], axis=0).astype(BF16)

    for swap in swaps:
        swap.wait_send()
    for k in range(1, nz):
        qz_copy(k).wait_send()
        z_copy(lax.rem(z + k, nz)).wait_send()
    for k in range(1, ny):
        for w in range(2):
            qy_copy(w, k).wait_send()
            y_copy(w, k).wait_send()


def per_device(ny, nz, queries, cache_keys, cache_values, new_keys, new_values, doc_start, doc_count):
    hbm = pl.BlockSpec(memory_space=pltpu.HBM)
    dma = pltpu.SemaphoreType.DMA
    half = nz // 2
    tiles = 2 * half + 1
    return pl.pallas_call(
        functools.partial(kernel, ny, nz),
        out_shape=pltpu.VMEM(queries.shape, BF16),
        in_specs=[hbm] * 7,
        out_specs=pl.BlockSpec(memory_space=pltpu.VMEM),
        scratch_shapes=[
            pltpu.VMEM(queries.shape, BF16),
            pltpu.VMEM(new_keys.shape, BF16),
            pltpu.VMEM(new_values.shape, BF16),
            pltpu.SMEM(doc_start.shape[::-1], jnp.int32),
            pltpu.SMEM(doc_count.shape[::-1], jnp.int32),
            pltpu.VMEM((ny, nz, 2, 16, 128), BF16),
            pltpu.VMEM((ny, nz, 16, 128), BF16),
            pltpu.VMEM((2, 2 * TOK, 128), BF16),
            pltpu.VMEM((2, 2 * TOK, 128), BF16),
            pltpu.VMEM((2, 512, 128), F32),
            pltpu.VMEM((2, 2 * TOK, 256), BF16),
            pltpu.VMEM((2, 2 * TOK, 256), BF16),
            pltpu.VMEM((2, 16 * half * ny, 2 * TOK), F32),
            pltpu.VMEM((2, ny, tiles, 16, 128), BF16),
            pltpu.VMEM((2, ny - 1, tiles, 16, 128), BF16),
            pltpu.VMEM((nz, 3, 16, 128), BF16),
            pltpu.VMEM((nz, 3, 16, 128), BF16),
            dma((7,)),
            dma((2,)), dma((2,)),
            dma((nz - 1,)), dma((nz,)),
            dma((2, ny - 1)), dma((2, ny - 1)),
            dma((2, ny - 1)), dma((2, ny - 1)),
            dma((nz,)), dma((nz,)),
        ],
        compiler_params=pltpu.CompilerParams(
            collective_id=0, has_side_effects=True, vmem_limit_bytes=60 * 1024 * 1024
        ),
        name="attention",
    )(
        queries,
        cache_keys.reshape(2 * TOK, 128),
        cache_values.reshape(2 * TOK, 128),
        new_keys,
        new_values,
        doc_start.T,
        doc_count.T,
    )


def solution(mesh):
    ny, nz = 4, mesh.shape["seq"] // 8
    placed = (P("seq", "kvh", None),) * 5 + (P(), P())
    return jax.shard_map(
        functools.partial(per_device, ny, nz),
        mesh=mesh,
        in_specs=placed,
        out_specs=P("seq", "kvh", None),
        check_vma=False,
    )
```

```python
import functools

import jax
import jax.numpy as jnp
from jax import lax
from jax.experimental import pallas as pl
from jax.experimental.pallas import tpu as pltpu
from jax.sharding import PartitionSpec as P

MESH = pl.DeviceIdType.MESH
HD = 128
BLOCK = 512
NBLOCKS = 4
TOK = BLOCK * NBLOCKS
NEG = -1e30
SCALE = HD ** (-0.5)
F32 = jnp.float32
BF16 = jnp.bfloat16


def lanes_of(rows):
    return lax.broadcasted_iota(jnp.int32, (rows, 128), 1)


def encode(stat, count):
    stat = jnp.where(lanes_of(16) < count, stat, 0.0)
    high = stat.astype(BF16).astype(F32)
    rest = stat - high
    middle = rest.astype(BF16).astype(F32)
    low = rest - middle
    return high + pltpu.roll(middle, 32, 1) + pltpu.roll(low, 64, 1)


def decode(tile):
    tile = tile.astype(F32)
    return tile + pltpu.roll(tile, 96, 1) + pltpu.roll(tile, 64, 1)


def weights_of(stats):
    top = functools.reduce(jnp.maximum, stats)
    raw = [jnp.exp(s - top) for s in stats]
    total = functools.reduce(jnp.add, raw)
    inverse = 1.0 / total
    return [w * inverse for w in raw], top + jnp.log(total)


def two_columns(weight, g, column):
    part = weight[g * 8 : (g + 1) * 8]
    return jnp.concatenate(
        [jnp.broadcast_to(part[:, column + r : column + r + 1], (8, 128)) for r in range(2)], axis=0
    )


def by_distance(n, first=1):
    return sorted(range(first, n), key=lambda k: -min(k, n - k))


def kernel(
    ny, nz,
    q_hbm, k_hbm, v_hbm, nk_hbm, nv_hbm, start_hbm, count_hbm, out_ref,
    q_ref, nk_ref, nv_ref, start_ref, count_ref,
    q_mine, qbuf, bias, kraw, vraw, temp, kaug, vaug, scores,
    y_out, y_in, z_out, z_in,
    load_sem, kv_send, kv_recv, qz_send, qz_recv, qy_send, qy_recv,
    y_send, y_recv, z_send, z_recv,
):
    half = nz // 2
    pair = half // 2
    seq = lax.axis_index("seq")
    x = lax.axis_index("kvh")
    core = lax.rem(seq, 2)
    z = lax.rem(lax.div(seq, 2), nz)
    y = lax.div(seq, 2 * nz)
    other = 1 - core
    hub = 1 - lax.div(z, half)
    is_hub = hub == core
    place = lax.rem(z, half)
    base = (1 - core) * half

    def device(yy, zz, cc):
        return ((yy * nz + zz) * 2 + cc, x)

    def along(i):
        return lax.rem(y + i, ny)

    def around(i):
        return lax.rem(z + i, nz)

    def remote(src, dst, send, recv, peer):
        return pltpu.make_async_remote_copy(
            src_ref=src, dst_ref=dst, send_sem=send, recv_sem=recv, device_id=peer, device_id_type=MESH
        )

    loads = [
        pltpu.make_async_copy(src, dst, load_sem.at[i])
        for i, (src, dst) in enumerate(
            [
                (q_hbm, q_ref), (start_hbm, start_ref), (count_hbm, count_ref),
                (k_hbm, kraw.at[0]), (v_hbm, vraw.at[0]), (nk_hbm, nk_ref), (nv_hbm, nv_ref),
            ]
        )
    ]
    for load in loads:
        load.start()

    barrier = pltpu.get_barrier_semaphore()

    def greet(peer):
        pl.semaphore_signal(barrier, inc=1, device_id=peer, device_id_type=MESH)

    for k in by_distance(nz):
        greet(device(y, around(k), hub))
    for i in range(half):
        greet(device(y, base + lax.rem(place + half - 1 - i, half), 1 - hub))
    for k in by_distance(ny):
        greet(device(along(k), z, core))

    @pl.when(hub != core)
    def _():
        greet(device(y, z, hub))

    loads[0].wait()
    q_own = q_ref[...].astype(F32)
    for g in range(2):
        q_mine[g] = jnp.concatenate([q_own[r, g * 8 : (g + 1) * 8] for r in range(2)], axis=0).astype(BF16)

    @pl.when(is_hub)
    def _():
        qbuf[y, place, core] = q_mine[...]

    pl.semaphore_wait(barrier, nz - 1 + half + ny - 1 + jnp.abs(hub - core))

    def qz_copy(k):
        return remote(
            q_mine, qbuf.at[y, place, core], qz_send.at[k], qz_recv.at[place, core], device(y, around(k), hub)
        )

    for k in by_distance(nz):
        qz_copy(k).start()

    @pl.when(hub != core)
    def _():
        qz_copy(0).start()

    swaps = [
        remote(src, dst, kv_send.at[i], kv_recv.at[i], device(y, z, other))
        for i, (src, dst) in enumerate([(k_hbm, kraw.at[1]), (v_hbm, vraw.at[1])])
    ]
    for swap in swaps:
        swap.start()

    lane = lanes_of(8)
    block = jnp.where(lane < NBLOCKS, seq * NBLOCKS + lane, (seq + 1 - 2 * core) * NBLOCKS + lane - NBLOCKS)

    def row_bias(row):
        seen = None
        for i in range(2):
            first = start_ref[i, row]
            inside = (block >= first) & (block < first + count_ref[i, row])
            seen = inside if seen is None else seen | inside
        return jnp.where(seen | (lane >= 2 * NBLOCKS), 0.0, NEG)

    def fill_bias(i, carry):
        yy, zi, cc = lax.div(i, nz), lax.rem(lax.div(i, 2), half), lax.rem(i, 2)
        row = 4 * (yy * nz + base + zi) + 2 * cc
        bias[yy, zi, cc] = jnp.concatenate([row_bias(row), row_bias(row + 1)], axis=0).astype(BF16)
        return carry

    loads[1].wait()
    loads[2].wait()
    lax.fori_loop(0, ny * nz, fill_bias, 0)

    piece = 256

    def split(which):
        def body(i, carry):
            at = pl.multiple_of(which * TOK + i * piece, piece)
            flat = pl.multiple_of(i * 2 * piece, 2 * piece)
            indicator = (lanes_of(piece) == lax.div(at, BLOCK)).astype(F32).astype(BF16)
            temp[0] = kraw[which, pl.ds(flat, 2 * piece), :].astype(F32)
            temp[1] = vraw[which, pl.ds(flat, 2 * piece), :].astype(F32)
            for g in range(2):
                kaug[g, pl.ds(at, piece), 0:128] = temp[0, pl.ds(g, piece, stride=2), :].astype(BF16)
                kaug[g, pl.ds(at, piece), 128:256] = indicator
                vaug[g, pl.ds(at, piece), 0:128] = temp[1, pl.ds(g, piece, stride=2), :].astype(BF16)
                vaug[g, pl.ds(at, piece), 128:256] = jnp.ones((piece, 128), BF16)
            return carry

        lax.fori_loop(0, TOK // piece, body, 0)

    loads[3].wait()
    loads[4].wait()
    split(0)

    def qy_copy(w, k):
        mine = qbuf.at[y, pl.ds(w * pair, pair)]
        return remote(mine, mine, qy_send.at[w, k - 1], qy_recv.at[w, k - 1], device(along(k), z, core))

    def qy_arrival(w, k):
        there = qbuf.at[along(ny - k), pl.ds(w * pair, pair)]
        return remote(there, there, qy_send.at[w, k - 1], qy_recv.at[w, k - 1], device(along(k), z, core))

    for w in range(2):
        for zi in range(w * pair, (w + 1) * pair):
            for cc in range(2):

                @pl.when((base + zi != z) | (core != cc))
                def _():
                    there = qbuf.at[y, zi, cc]
                    remote(
                        there, there, qz_send.at[0], qz_recv.at[zi, cc], device(along(1), z, core)
                    ).wait_recv()

        for k in by_distance(ny):
            qy_copy(w, k).start()

    for swap in swaps:
        swap.wait_recv()
    split(1)

    rows = 32 * pair
    count = 4 * pair

    def attend(w):
        tops = []
        for g in range(2):
            lhs = jnp.concatenate(
                [
                    qbuf[:, pl.ds(w * pair, pair), :, g].reshape(ny * rows, 128),
                    bias[:, pl.ds(w * pair, pair)].reshape(ny * rows, 128),
                ],
                axis=1,
            )
            top = None
            for b in range(2 * NBLOCKS):
                s = lax.dot_general(
                    lhs, kaug[g, b * BLOCK : (b + 1) * BLOCK, :], (((1,), (1,)), ((), ())),
                    preferred_element_type=F32,
                )
                scores[g, :, b * BLOCK : (b + 1) * BLOCK] = s
                for i in range(BLOCK // 128):
                    part = s[:, i * 128 : (i + 1) * 128]
                    top = part if top is None else jnp.maximum(top, part)
            tops.append(jnp.max(top, axis=1, keepdims=True))
        stats = [[None] * 2 for _ in range(ny)]
        for g in range(2):
            total = None
            for b in range(2 * NBLOCKS):
                s = scores[g, :, b * BLOCK : (b + 1) * BLOCK]
                p = jnp.exp((s - tops[g]) * SCALE).astype(BF16)
                term = jnp.dot(p, vaug[g, b * BLOCK : (b + 1) * BLOCK, :], preferred_element_type=F32)
                total = term if total is None else total + term
            norm = total[:, 128:256]
            out = total[:, 0:128] * (1.0 / norm)
            stat = tops[g] * SCALE + jnp.log(norm)
            for yy in range(ny):
                packed = jnp.zeros((8, 128), F32)
                for k in range(count):
                    at = yy * rows + k * 8
                    packed = jnp.where(lane == k, stat[at : at + 8], packed)
                stats[yy][g] = packed
                for i in range(count // 2):
                    at = yy * rows + i * 16
                    y_out[w, yy, i * 2 + g] = out[at : at + 16].astype(BF16)
        for yy in range(ny):
            y_out[w, yy, count] = encode(jnp.concatenate(stats[yy], axis=0), count).astype(BF16)

    def y_copy(w, k):
        return remote(
            y_out.at[w, along(k)], y_in.at[w, k - 1], y_send.at[w, k - 1], y_recv.at[w, k - 1],
            device(along(k), z, core),
        )

    def forward(w, carry):
        for k in range(1, ny):
            qy_arrival(w, k).wait_recv()
        attend(w)
        for k in by_distance(ny):
            y_copy(w, k).start()
        return carry

    lax.fori_loop(0, 2, forward, 0)

    def z_copy(zi, cc):
        return remote(
            z_out.at[zi, cc], z_in.at[z], z_send.at[zi, cc], z_recv.at[z], device(y, base + zi, cc)
        )

    def back(w, carry):
        for k in range(1, ny):
            y_copy(w, k).wait_recv()
        parts = [y_out.at[w, y]] + [y_in.at[w, k] for k in range(ny - 1)]
        weights, stat = weights_of([decode(part[count]) for part in parts])
        stat = encode(stat, count)
        for i in range(count // 2):
            zi, cc = w * pair + i // 2, i % 2
            for g in range(2):
                tile = None
                for part, weight in zip(parts, weights):
                    term = part[i * 2 + g].astype(F32) * two_columns(weight, g, 2 * i)
                    tile = term if tile is None else tile + term
                z_out[zi, cc, g] = tile.astype(BF16)
            z_out[zi, cc, 2] = (stat if i == 0 else pltpu.roll(stat, 128 - 2 * i, 1)).astype(BF16)
        for i in range(count // 2):
            zi, cc = w * pair + i // 2, i % 2

            @pl.when((base + zi != z) | (core != cc))
            def _():
                z_copy(zi, cc).start()

        return carry

    lax.fori_loop(0, 2, back, 0)

    loads[5].wait()
    loads[6].wait()

    @pl.when(is_hub)
    def _():
        z_in[z] = z_out[place, core]

    own = [None, None]
    for g in range(2):
        packed = jnp.zeros((8, 128), F32)
        for r in range(2):
            key = nk_ref[r].astype(F32)[g : g + 1]
            dots = jnp.sum(q_own[r, g * 8 : (g + 1) * 8] * key, axis=1, keepdims=True) * SCALE
            packed = jnp.where(lane == r, dots, packed)
        own[g] = packed
    own = jnp.concatenate(own, axis=0)

    for k in range(nz):
        zz = around(k)

        @pl.when((hub != core) | (zz != z))
        def _():
            there = z_in.at[zz]
            remote(there, there, z_send.at[0, 0], z_recv.at[zz], device(along(1), z, core)).wait_recv()

    parts = [z_in.at[k] for k in range(nz)]
    weights, _ = weights_of([decode(part[2]) for part in parts] + [own])
    tiles = []
    for g in range(2):
        tile = None
        for part, weight in zip(parts, weights):
            term = part[g].astype(F32) * two_columns(weight, g, 0)
            tile = term if tile is None else tile + term
        value = jnp.concatenate(
            [jnp.broadcast_to(nv_ref[r].astype(F32)[g : g + 1], (8, 128)) for r in range(2)], axis=0
        )
        tiles.append(tile + value * two_columns(weights[-1], g, 0))
    for r in range(2):
        out_ref[r] = jnp.concatenate([tiles[g][r * 8 : (r + 1) * 8] for g in range(2)], axis=0).astype(BF16)

    for swap in swaps:
        swap.wait_send()
    for k in range(1, nz):
        qz_copy(k).wait_send()

    @pl.when(hub != core)
    def _():
        qz_copy(0).wait_send()

    for zi in range(half):
        for cc in range(2):

            @pl.when((base + zi != z) | (core != cc))
            def _():
                z_copy(zi, cc).wait_send()

    for k in range(1, ny):
        for w in range(2):
            qy_copy(w, k).wait_send()
            y_copy(w, k).wait_send()


def per_device(ny, nz, queries, cache_keys, cache_values, new_keys, new_values, doc_start, doc_count):
    hbm = pl.BlockSpec(memory_space=pltpu.HBM)
    dma = pltpu.SemaphoreType.DMA
    half = nz // 2
    pair = half // 2
    tiles = 4 * pair + 1
    return pl.pallas_call(
        functools.partial(kernel, ny, nz),
        out_shape=pltpu.VMEM(queries.shape, BF16),
        in_specs=[hbm] * 7,
        out_specs=pl.BlockSpec(memory_space=pltpu.VMEM),
        scratch_shapes=[
            pltpu.VMEM(queries.shape, BF16),
            pltpu.VMEM(new_keys.shape, BF16),
            pltpu.VMEM(new_values.shape, BF16),
            pltpu.SMEM(doc_start.shape[::-1], jnp.int32),
            pltpu.SMEM(doc_count.shape[::-1], jnp.int32),
            pltpu.VMEM((2, 16, 128), BF16),
            pltpu.VMEM((ny, half, 2, 2, 16, 128), BF16),
            pltpu.VMEM((ny, half, 2, 16, 128), BF16),
            pltpu.VMEM((2, 2 * TOK, 128), BF16),
            pltpu.VMEM((2, 2 * TOK, 128), BF16),
            pltpu.VMEM((2, 512, 128), F32),
            pltpu.VMEM((2, 2 * TOK, 256), BF16),
            pltpu.VMEM((2, 2 * TOK, 256), BF16),
            pltpu.VMEM((2, 32 * pair * ny, 2 * TOK), F32),
            pltpu.VMEM((2, ny, tiles, 16, 128), BF16),
            pltpu.VMEM((2, ny - 1, tiles, 16, 128), BF16),
            pltpu.VMEM((half, 2, 3, 16, 128), BF16),
            pltpu.VMEM((nz, 3, 16, 128), BF16),
            dma((7,)),
            dma((2,)), dma((2,)),
            dma((nz,)), dma((half, 2)),
            dma((2, ny - 1)), dma((2, ny - 1)),
            dma((2, ny - 1)), dma((2, ny - 1)),
            dma((half, 2)), dma((nz,)),
        ],
        compiler_params=pltpu.CompilerParams(
            collective_id=0, has_side_effects=True, vmem_limit_bytes=60 * 1024 * 1024
        ),
        name="attention",
    )(
        queries,
        cache_keys.reshape(2 * TOK, 128),
        cache_values.reshape(2 * TOK, 128),
        new_keys,
        new_values,
        doc_start.T,
        doc_count.T,
    )


def solution(mesh):
    ny, nz = 4, mesh.shape["seq"] // 8
    placed = (P("seq", "kvh", None),) * 5 + (P(), P())
    return jax.shard_map(
        functools.partial(per_device, ny, nz),
        mesh=mesh,
        in_specs=placed,
        out_specs=P("seq", "kvh", None),
        check_vma=False,
    )
```

```python
import functools

import jax
import jax.numpy as jnp
from jax import lax
from jax.experimental import pallas as pl
from jax.experimental.pallas import tpu as pltpu
from jax.sharding import PartitionSpec as P

MESH = pl.DeviceIdType.MESH
HD = 128
BLOCK = 512
NBLOCKS = 4
TOK = BLOCK * NBLOCKS
NEG = -1e30
SCALE = HD ** (-0.5)
F32 = jnp.float32
BF16 = jnp.bfloat16


def lanes_of(rows):
    return lax.broadcasted_iota(jnp.int32, (rows, 128), 1)


def encode(stat, count):
    stat = jnp.where(lanes_of(16) < count, stat, 0.0)
    high = stat.astype(BF16).astype(F32)
    rest = stat - high
    middle = rest.astype(BF16).astype(F32)
    low = rest - middle
    return high + pltpu.roll(middle, 32, 1) + pltpu.roll(low, 64, 1)


def decode(tile):
    tile = tile.astype(F32)
    return tile + pltpu.roll(tile, 96, 1) + pltpu.roll(tile, 64, 1)


def weights_of(stats):
    top = functools.reduce(jnp.maximum, stats)
    raw = [jnp.exp(s - top) for s in stats]
    total = functools.reduce(jnp.add, raw)
    inverse = 1.0 / total
    return [w * inverse for w in raw], top + jnp.log(total)


def two_columns(weight, g, column):
    part = weight[g * 8 : (g + 1) * 8]
    return jnp.concatenate(
        [jnp.broadcast_to(part[:, column + r : column + r + 1], (8, 128)) for r in range(2)], axis=0
    )


def by_distance(n, first=1):
    return sorted(range(first, n), key=lambda k: -min(k, n - k))


def kernel(
    ny, nz,
    q_hbm, k_hbm, v_hbm, nk_hbm, nv_hbm, start_hbm, count_hbm, out_ref,
    q_ref, nk_ref, nv_ref, start_ref, count_ref,
    q_mine, qbuf, bias, kraw, vraw, temp, kaug, vaug, scores,
    y_out, y_in, z_out, z_in,
    load_sem, kv_send, kv_recv, qz_send, qz_recv, qy_send, qy_recv,
    y_send, y_recv, z_send, z_recv,
):
    half = nz // 2
    pair = half // 2
    seq = lax.axis_index("seq")
    x = lax.axis_index("kvh")
    core = lax.rem(seq, 2)
    z = lax.rem(lax.div(seq, 2), nz)
    y = lax.div(seq, 2 * nz)
    other = 1 - core
    hub = 1 - lax.div(z, half)
    is_hub = hub == core
    place = lax.rem(z, half)
    base = (1 - core) * half

    def device(yy, zz, cc):
        return ((yy * nz + zz) * 2 + cc, x)

    def along(i):
        return lax.rem(y + i, ny)

    def around(i):
        return lax.rem(z + i, nz)

    def remote(src, dst, send, recv, peer):
        return pltpu.make_async_remote_copy(
            src_ref=src, dst_ref=dst, send_sem=send, recv_sem=recv, device_id=peer, device_id_type=MESH
        )

    loads = [
        pltpu.make_async_copy(src, dst, load_sem.at[i])
        for i, (src, dst) in enumerate(
            [
                (q_hbm, q_ref), (start_hbm, start_ref), (count_hbm, count_ref),
                (k_hbm, kraw.at[0]), (v_hbm, vraw.at[0]), (nk_hbm, nk_ref), (nv_hbm, nv_ref),
            ]
        )
    ]
    loads[0].start()

    barrier = pltpu.get_barrier_semaphore()

    def greet(peer):
        pl.semaphore_signal(barrier, inc=1, device_id=peer, device_id_type=MESH)

    for k in by_distance(nz):
        zz = around(k)
        greet(device(y, zz, hub))

        @pl.when(lax.div(zz, half) == 1 - core)
        def _():
            greet(device(y, zz, 1 - hub))

    for k in by_distance(ny):
        greet(device(along(k), z, core))
    greet(device(y, z, other))
    for load in loads[1:]:
        load.start()

    loads[0].wait()
    q_own = q_ref[...].astype(F32)
    for g in range(2):
        q_mine[g] = jnp.concatenate([q_own[r, g * 8 : (g + 1) * 8] for r in range(2)], axis=0).astype(BF16)

    @pl.when(is_hub)
    def _():
        qbuf[y, place, core] = q_mine[...]

    pl.semaphore_wait(barrier, nz - 1 + half + ny - 1 + jnp.abs(hub - core))

    def qz_copy(k):
        return remote(
            q_mine, qbuf.at[y, place, core], qz_send.at[k], qz_recv.at[place, core], device(y, around(k), hub)
        )

    for k in by_distance(nz):
        qz_copy(k).start()

    @pl.when(hub != core)
    def _():
        qz_copy(0).start()

    swaps = [
        remote(src, dst, kv_send.at[i], kv_recv.at[i], device(y, z, other))
        for i, (src, dst) in enumerate([(k_hbm, kraw.at[1]), (v_hbm, vraw.at[1])])
    ]
    for swap in swaps:
        swap.start()

    lane = lanes_of(8)
    block = jnp.where(lane < NBLOCKS, seq * NBLOCKS + lane, (seq + 1 - 2 * core) * NBLOCKS + lane - NBLOCKS)

    def row_bias(row):
        seen = None
        for i in range(2):
            first = start_ref[i, row]
            inside = (block >= first) & (block < first + count_ref[i, row])
            seen = inside if seen is None else seen | inside
        return jnp.where(seen | (lane >= 2 * NBLOCKS), 0.0, NEG)

    def fill_bias(i, carry):
        yy, zi, cc = lax.div(i, nz), lax.rem(lax.div(i, 2), half), lax.rem(i, 2)
        row = 4 * (yy * nz + base + zi) + 2 * cc
        bias[yy, zi, cc] = jnp.concatenate([row_bias(row), row_bias(row + 1)], axis=0).astype(BF16)
        return carry

    loads[1].wait()
    loads[2].wait()
    lax.fori_loop(0, ny * nz, fill_bias, 0)

    piece = 256

    def split(which):
        def body(i, carry):
            at = pl.multiple_of(which * TOK + i * piece, piece)
            flat = pl.multiple_of(i * 2 * piece, 2 * piece)
            indicator = (lanes_of(piece) == lax.div(at, BLOCK)).astype(F32).astype(BF16)
            temp[0] = kraw[which, pl.ds(flat, 2 * piece), :].astype(F32)
            temp[1] = vraw[which, pl.ds(flat, 2 * piece), :].astype(F32)
            for g in range(2):
                kaug[g, pl.ds(at, piece), 0:128] = temp[0, pl.ds(g, piece, stride=2), :].astype(BF16)
                kaug[g, pl.ds(at, piece), 128:256] = indicator
                vaug[g, pl.ds(at, piece), 0:128] = temp[1, pl.ds(g, piece, stride=2), :].astype(BF16)
                vaug[g, pl.ds(at, piece), 128:256] = jnp.ones((piece, 128), BF16)
            return carry

        lax.fori_loop(0, TOK // piece, body, 0)

    loads[3].wait()
    loads[4].wait()
    split(0)

    def qy_copy(w, k):
        mine = qbuf.at[y, pl.ds(w * pair, pair)]
        return remote(mine, mine, qy_send.at[w, k - 1], qy_recv.at[w, k - 1], device(along(k), z, core))

    def qy_arrival(w, k):
        there = qbuf.at[along(ny - k), pl.ds(w * pair, pair)]
        return remote(there, there, qy_send.at[w, k - 1], qy_recv.at[w, k - 1], device(along(k), z, core))

    for w in range(2):
        for zi in range(w * pair, (w + 1) * pair):
            for cc in range(2):

                @pl.when((base + zi != z) | (core != cc))
                def _():
                    there = qbuf.at[y, zi, cc]
                    remote(
                        there, there, qz_send.at[0], qz_recv.at[zi, cc], device(along(1), z, core)
                    ).wait_recv()

        for k in by_distance(ny):
            qy_copy(w, k).start()

    for swap in swaps:
        swap.wait_recv()
    split(1)

    rows = 32 * pair
    count = 4 * pair

    def attend(w):
        tops = []
        for g in range(2):
            lhs = jnp.concatenate(
                [
                    qbuf[:, pl.ds(w * pair, pair), :, g].reshape(ny * rows, 128),
                    bias[:, pl.ds(w * pair, pair)].reshape(ny * rows, 128),
                ],
                axis=1,
            )
            top = None
            for b in range(2 * NBLOCKS):
                s = lax.dot_general(
                    lhs, kaug[g, b * BLOCK : (b + 1) * BLOCK, :], (((1,), (1,)), ((), ())),
                    preferred_element_type=F32,
                )
                scores[g, :, b * BLOCK : (b + 1) * BLOCK] = s
                for i in range(BLOCK // 128):
                    part = s[:, i * 128 : (i + 1) * 128]
                    top = part if top is None else jnp.maximum(top, part)
            tops.append(jnp.max(top, axis=1, keepdims=True))
        stats = [[None] * 2 for _ in range(ny)]
        for g in range(2):
            total = None
            for b in range(2 * NBLOCKS):
                s = scores[g, :, b * BLOCK : (b + 1) * BLOCK]
                p = jnp.exp((s - tops[g]) * SCALE).astype(BF16)
                term = jnp.dot(p, vaug[g, b * BLOCK : (b + 1) * BLOCK, :], preferred_element_type=F32)
                total = term if total is None else total + term
            norm = total[:, 128:256]
            out = total[:, 0:128] * (1.0 / norm)
            stat = tops[g] * SCALE + jnp.log(norm)
            for yy in range(ny):
                packed = jnp.zeros((8, 128), F32)
                for k in range(count):
                    at = yy * rows + k * 8
                    packed = jnp.where(lane == k, stat[at : at + 8], packed)
                stats[yy][g] = packed
                for i in range(count // 2):
                    at = yy * rows + i * 16
                    y_out[w, yy, i * 2 + g] = out[at : at + 16].astype(BF16)
        for yy in range(ny):
            y_out[w, yy, count] = encode(jnp.concatenate(stats[yy], axis=0), count).astype(BF16)

    def y_copy(w, yy):
        return remote(
            y_out.at[w, yy], y_in.at[w, y], y_send.at[w, yy], y_recv.at[w, y], device(yy, z, core)
        )

    def forward(w, carry):
        for k in range(1, ny):
            qy_arrival(w, k).wait_recv()
        attend(w)
        for yy in range(ny):

            @pl.when(yy != y)
            def _():
                y_copy(w, yy).start()

        return carry

    lax.fori_loop(0, 2, forward, 0)

    def z_copy(zi, cc):
        return remote(
            z_out.at[zi, cc], z_in.at[z], z_send.at[zi, cc], z_recv.at[z], device(y, base + zi, cc)
        )

    def back(w, carry):
        for k in range(1, ny):
            there = y_in.at[w, along(k)]
            remote(there, there, y_send.at[w, 0], y_recv.at[w, along(k)], device(along(k), z, core)).wait_recv()
        parts = [y_out.at[w, y]] + [y_in.at[w, along(k)] for k in range(1, ny)]
        weights, stat = weights_of([decode(part[count]) for part in parts])
        stat = encode(stat, count)
        for i in range(count // 2):
            zi, cc = w * pair + i // 2, i % 2
            for g in range(2):
                tile = None
                for part, weight in zip(parts, weights):
                    term = part[i * 2 + g].astype(F32) * two_columns(weight, g, 2 * i)
                    tile = term if tile is None else tile + term
                z_out[zi, cc, g] = tile.astype(BF16)
            z_out[zi, cc, 2] = (stat if i == 0 else pltpu.roll(stat, 128 - 2 * i, 1)).astype(BF16)
        for i in range(count // 2):
            zi, cc = w * pair + i // 2, i % 2

            @pl.when((base + zi != z) | (core != cc))
            def _():
                z_copy(zi, cc).start()

        return carry

    lax.fori_loop(0, 2, back, 0)

    loads[5].wait()
    loads[6].wait()

    @pl.when(is_hub)
    def _():
        z_in[z] = z_out[place, core]

    own = [None, None]
    for g in range(2):
        packed = jnp.zeros((8, 128), F32)
        for r in range(2):
            key = nk_ref[r].astype(F32)[g : g + 1]
            dots = jnp.sum(q_own[r, g * 8 : (g + 1) * 8] * key, axis=1, keepdims=True) * SCALE
            packed = jnp.where(lane == r, dots, packed)
        own[g] = packed
    own = jnp.concatenate(own, axis=0)

    for k in range(nz):
        zz = around(k)

        @pl.when((hub != core) | (zz != z))
        def _():
            there = z_in.at[zz]
            remote(there, there, z_send.at[0, 0], z_recv.at[zz], device(along(1), z, core)).wait_recv()

    parts = [z_in.at[k] for k in range(nz)]
    weights, _ = weights_of([decode(part[2]) for part in parts] + [own])
    tiles = []
    for g in range(2):
        tile = None
        for part, weight in zip(parts, weights):
            term = part[g].astype(F32) * two_columns(weight, g, 0)
            tile = term if tile is None else tile + term
        value = jnp.concatenate(
            [jnp.broadcast_to(nv_ref[r].astype(F32)[g : g + 1], (8, 128)) for r in range(2)], axis=0
        )
        tiles.append(tile + value * two_columns(weights[-1], g, 0))
    for r in range(2):
        out_ref[r] = jnp.concatenate([tiles[g][r * 8 : (r + 1) * 8] for g in range(2)], axis=0).astype(BF16)

    for swap in swaps:
        swap.wait_send()
    for k in range(1, nz):
        qz_copy(k).wait_send()

    @pl.when(hub != core)
    def _():
        qz_copy(0).wait_send()

    for zi in range(half):
        for cc in range(2):

            @pl.when((base + zi != z) | (core != cc))
            def _():
                z_copy(zi, cc).wait_send()

    for k in range(1, ny):
        for w in range(2):
            qy_copy(w, k).wait_send()
            y_copy(w, along(k)).wait_send()


def per_device(ny, nz, queries, cache_keys, cache_values, new_keys, new_values, doc_start, doc_count):
    hbm = pl.BlockSpec(memory_space=pltpu.HBM)
    dma = pltpu.SemaphoreType.DMA
    half = nz // 2
    pair = half // 2
    tiles = 4 * pair + 1
    return pl.pallas_call(
        functools.partial(kernel, ny, nz),
        out_shape=pltpu.VMEM(queries.shape, BF16),
        in_specs=[hbm] * 7,
        out_specs=pl.BlockSpec(memory_space=pltpu.VMEM),
        scratch_shapes=[
            pltpu.VMEM(queries.shape, BF16),
            pltpu.VMEM(new_keys.shape, BF16),
            pltpu.VMEM(new_values.shape, BF16),
            pltpu.SMEM(doc_start.shape[::-1], jnp.int32),
            pltpu.SMEM(doc_count.shape[::-1], jnp.int32),
            pltpu.VMEM((2, 16, 128), BF16),
            pltpu.VMEM((ny, half, 2, 2, 16, 128), BF16),
            pltpu.VMEM((ny, half, 2, 16, 128), BF16),
            pltpu.VMEM((2, 2 * TOK, 128), BF16),
            pltpu.VMEM((2, 2 * TOK, 128), BF16),
            pltpu.VMEM((2, 512, 128), F32),
            pltpu.VMEM((2, 2 * TOK, 256), BF16),
            pltpu.VMEM((2, 2 * TOK, 256), BF16),
            pltpu.VMEM((2, 32 * pair * ny, 2 * TOK), F32),
            pltpu.VMEM((2, ny, tiles, 16, 128), BF16),
            pltpu.VMEM((2, ny, tiles, 16, 128), BF16),
            pltpu.VMEM((half, 2, 3, 16, 128), BF16),
            pltpu.VMEM((nz, 3, 16, 128), BF16),
            dma((7,)),
            dma((2,)), dma((2,)),
            dma((nz,)), dma((half, 2)),
            dma((2, ny - 1)), dma((2, ny - 1)),
            dma((2, ny)), dma((2, ny)),
            dma((half, 2)), dma((nz,)),
        ],
        compiler_params=pltpu.CompilerParams(
            collective_id=0, has_side_effects=True, vmem_limit_bytes=60 * 1024 * 1024
        ),
        name="attention",
    )(
        queries,
        cache_keys.reshape(2 * TOK, 128),
        cache_values.reshape(2 * TOK, 128),
        new_keys,
        new_values,
        doc_start.T,
        doc_count.T,
    )


def solution(mesh):
    ny, nz = 4, mesh.shape["seq"] // 8
    placed = (P("seq", "kvh", None),) * 5 + (P(), P())
    return jax.shard_map(
        functools.partial(per_device, ny, nz),
        mesh=mesh,
        in_specs=placed,
        out_specs=P("seq", "kvh", None),
        check_vma=False,
    )
```

```python
import functools

import jax
import jax.numpy as jnp
from jax import lax
from jax.experimental import pallas as pl
from jax.experimental.pallas import tpu as pltpu
from jax.sharding import PartitionSpec as P

MESH = pl.DeviceIdType.MESH
HD = 128
BLOCK = 512
NBLOCKS = 4
TOK = BLOCK * NBLOCKS
NEG = -1e30
SCALE = HD ** (-0.5)
F32 = jnp.float32
BF16 = jnp.bfloat16


def lanes_of(rows):
    return lax.broadcasted_iota(jnp.int32, (rows, 128), 1)


def encode(stat, count):
    stat = jnp.where(lanes_of(16) < count, stat, 0.0)
    high = stat.astype(BF16).astype(F32)
    rest = stat - high
    middle = rest.astype(BF16).astype(F32)
    low = rest - middle
    return high + pltpu.roll(middle, 32, 1) + pltpu.roll(low, 64, 1)


def decode(tile):
    tile = tile.astype(F32)
    return tile + pltpu.roll(tile, 96, 1) + pltpu.roll(tile, 64, 1)


def weights_of(stats):
    top = functools.reduce(jnp.maximum, stats)
    raw = [jnp.exp(s - top) for s in stats]
    total = functools.reduce(jnp.add, raw)
    inverse = 1.0 / total
    return [w * inverse for w in raw], top + jnp.log(total)


def two_columns(weight, g, column):
    part = weight[g * 8 : (g + 1) * 8]
    return jnp.concatenate(
        [jnp.broadcast_to(part[:, column + r : column + r + 1], (8, 128)) for r in range(2)], axis=0
    )


def by_distance(n, first=1):
    return sorted(range(first, n), key=lambda k: -min(k, n - k))


def kernel(
    ny, nz,
    q_hbm, k_hbm, v_hbm, nk_hbm, nv_hbm, start_hbm, count_hbm, out_ref,
    q_ref, nk_ref, nv_ref, start_ref, count_ref,
    q_mine, qbuf, bias, kraw, vraw, temp, kaug, vaug, scores,
    y_out, y_in, z_out, z_in,
    load_sem, kv_send, kv_recv, qz_send, qz_recv, qy_send, qy_recv,
    y_send, y_recv, z_send, z_recv,
):
    half = nz // 2
    pair = half // 2
    seq = lax.axis_index("seq")
    x = lax.axis_index("kvh")
    core = lax.rem(seq, 2)
    z = lax.rem(lax.div(seq, 2), nz)
    y = lax.div(seq, 2 * nz)
    other = 1 - core
    hub = 1 - lax.div(z, half)
    is_hub = hub == core
    place = lax.rem(z, half)
    base = (1 - core) * half

    def device(yy, zz, cc):
        return ((yy * nz + zz) * 2 + cc, x)

    def along(i):
        return lax.rem(y + i, ny)

    def around(i):
        return lax.rem(z + i, nz)

    def remote(src, dst, send, recv, peer):
        return pltpu.make_async_remote_copy(
            src_ref=src, dst_ref=dst, send_sem=send, recv_sem=recv, device_id=peer, device_id_type=MESH
        )

    loads = [
        pltpu.make_async_copy(src, dst, load_sem.at[i])
        for i, (src, dst) in enumerate(
            [
                (q_hbm, q_ref), (start_hbm, start_ref), (count_hbm, count_ref),
                (k_hbm, kraw.at[0]), (v_hbm, vraw.at[0]), (nk_hbm, nk_ref), (nv_hbm, nv_ref),
            ]
        )
    ]
    loads[0].start()

    barrier = pltpu.get_barrier_semaphore()

    def greet(peer):
        pl.semaphore_signal(barrier, inc=1, device_id=peer, device_id_type=MESH)

    for k in by_distance(nz):
        zz = around(k)
        greet(device(y, zz, hub))

        @pl.when(lax.div(zz, half) == 1 - core)
        def _():
            greet(device(y, zz, 1 - hub))

    for k in by_distance(ny):
        greet(device(along(k), z, core))
    greet(device(y, z, other))
    for load in loads[1:]:
        load.start()

    loads[0].wait()
    q_own = q_ref[...].astype(F32)
    for g in range(2):
        q_mine[g] = jnp.concatenate([q_own[r, g * 8 : (g + 1) * 8] for r in range(2)], axis=0).astype(BF16)

    @pl.when(is_hub)
    def _():
        qbuf[y, place, core] = q_mine[...]

    pl.semaphore_wait(barrier, nz - 1 + half + ny - 1 + jnp.abs(hub - core))

    def qz_copy(k):
        return remote(
            q_mine, qbuf.at[y, place, core], qz_send.at[k], qz_recv.at[place, core], device(y, around(k), hub)
        )

    for k in by_distance(nz):
        qz_copy(k).start()

    @pl.when(hub != core)
    def _():
        qz_copy(0).start()

    swaps = [
        remote(src, dst, kv_send.at[i], kv_recv.at[i], device(y, z, other))
        for i, (src, dst) in enumerate([(k_hbm, kraw.at[1]), (v_hbm, vraw.at[1])])
    ]
    for swap in swaps:
        swap.start()

    lane = lanes_of(8)
    block = jnp.where(lane < NBLOCKS, seq * NBLOCKS + lane, (seq + 1 - 2 * core) * NBLOCKS + lane - NBLOCKS)

    def row_bias(row):
        seen = None
        for i in range(2):
            first = start_ref[i, row]
            inside = (block >= first) & (block < first + count_ref[i, row])
            seen = inside if seen is None else seen | inside
        return jnp.where(seen | (lane >= 2 * NBLOCKS), 0.0, NEG)

    def fill_bias(i, carry):
        yy, zi, cc = lax.div(i, nz), lax.rem(lax.div(i, 2), half), lax.rem(i, 2)
        row = 4 * (yy * nz + base + zi) + 2 * cc
        bias[yy, zi, cc] = jnp.concatenate([row_bias(row), row_bias(row + 1)], axis=0).astype(BF16)
        return carry

    loads[1].wait()
    loads[2].wait()
    lax.fori_loop(0, ny * nz, fill_bias, 0)

    piece = 256

    def split(which):
        def body(i, carry):
            at = pl.multiple_of(which * TOK + i * piece, piece)
            flat = pl.multiple_of(i * 2 * piece, 2 * piece)
            indicator = (lanes_of(piece) == lax.div(at, BLOCK)).astype(F32).astype(BF16)
            temp[0, 0 : 2 * piece] = kraw[which, pl.ds(flat, 2 * piece), :].astype(F32)
            temp[1, 0 : 2 * piece] = vraw[which, pl.ds(flat, 2 * piece), :].astype(F32)
            for g in range(2):
                kaug[g, pl.ds(at, piece), 0:128] = temp[0, pl.ds(g, piece, stride=2), :].astype(BF16)
                kaug[g, pl.ds(at, piece), 128:256] = indicator
                vaug[g, pl.ds(at, piece), 0:128] = temp[1, pl.ds(g, piece, stride=2), :].astype(BF16)
                vaug[g, pl.ds(at, piece), 128:256] = jnp.ones((piece, 128), BF16)
            return carry

        lax.fori_loop(0, TOK // piece, body, 0)

    loads[3].wait()
    loads[4].wait()
    split(0)

    def qy_copy(w, k):
        mine = qbuf.at[y, pl.ds(w * pair, pair)]
        return remote(mine, mine, qy_send.at[w, k - 1], qy_recv.at[w, k - 1], device(along(k), z, core))

    def qy_arrival(w, k):
        there = qbuf.at[along(ny - k), pl.ds(w * pair, pair)]
        return remote(there, there, qy_send.at[w, k - 1], qy_recv.at[w, k - 1], device(along(k), z, core))

    for w in range(2):
        for zi in range(w * pair, (w + 1) * pair):
            for cc in range(2):

                @pl.when((base + zi != z) | (core != cc))
                def _():
                    there = qbuf.at[y, zi, cc]
                    remote(
                        there, there, qz_send.at[0], qz_recv.at[zi, cc], device(along(1), z, core)
                    ).wait_recv()

        for k in by_distance(ny):
            qy_copy(w, k).start()

    for swap in swaps:
        swap.wait_recv()
    split(1)

    rows = 32 * pair
    count = 4 * pair

    def attend(w):
        tops = []
        for g in range(2):
            lhs = jnp.concatenate(
                [
                    qbuf[:, pl.ds(w * pair, pair), :, g].reshape(ny * rows, 128),
                    bias[:, pl.ds(w * pair, pair)].reshape(ny * rows, 128),
                ],
                axis=1,
            )
            top = None
            for b in range(2 * NBLOCKS):
                s = lax.dot_general(
                    lhs, kaug[g, b * BLOCK : (b + 1) * BLOCK, :], (((1,), (1,)), ((), ())),
                    preferred_element_type=F32,
                )
                scores[g, :, b * BLOCK : (b + 1) * BLOCK] = s
                for i in range(BLOCK // 128):
                    part = s[:, i * 128 : (i + 1) * 128]
                    top = part if top is None else jnp.maximum(top, part)
            tops.append(jnp.max(top, axis=1, keepdims=True))
        stats = [[None] * 2 for _ in range(ny)]
        for g in range(2):
            total = None
            for b in range(2 * NBLOCKS):
                s = scores[g, :, b * BLOCK : (b + 1) * BLOCK]
                p = jnp.exp((s - tops[g]) * SCALE).astype(BF16)
                term = jnp.dot(p, vaug[g, b * BLOCK : (b + 1) * BLOCK, :], preferred_element_type=F32)
                total = term if total is None else total + term
            norm = total[:, 128:256]
            out = total[:, 0:128] * (1.0 / norm)
            stat = tops[g] * SCALE + jnp.log(norm)
            for yy in range(ny):
                packed = jnp.zeros((8, 128), F32)
                for k in range(count):
                    at = yy * rows + k * 8
                    packed = jnp.where(lane == k, stat[at : at + 8], packed)
                stats[yy][g] = packed
                for i in range(count // 2):
                    at = yy * rows + i * 16
                    y_out[w, yy, i * 2 + g] = out[at : at + 16].astype(BF16)
        for yy in range(ny):
            y_out[w, yy, count] = encode(jnp.concatenate(stats[yy], axis=0), count).astype(BF16)

    def y_copy(w, yy):
        return remote(
            y_out.at[w, yy], y_in.at[w, y], y_send.at[w, yy], y_recv.at[w, y], device(yy, z, core)
        )

    def forward(w, carry):
        for k in range(1, ny):
            qy_arrival(w, k).wait_recv()
        attend(w)
        for yy in range(ny):

            @pl.when(yy != y)
            def _():
                y_copy(w, yy).start()

        return carry

    lax.fori_loop(0, 2, forward, 0)

    def z_copy(zi, cc):
        return remote(
            z_out.at[zi, cc], z_in.at[z], z_send.at[zi, cc], z_recv.at[z], device(y, base + zi, cc)
        )

    def back(w, carry):
        for k in range(1, ny):
            there = y_in.at[w, along(k)]
            remote(there, there, y_send.at[w, 0], y_recv.at[w, along(k)], device(along(k), z, core)).wait_recv()
        parts = [y_out.at[w, y]] + [y_in.at[w, along(k)] for k in range(1, ny)]
        weights, stat = weights_of([decode(part[count]) for part in parts])
        stat = encode(stat, count)
        for i in range(count // 2):
            zi, cc = w * pair + i // 2, i % 2
            for g in range(2):
                tile = None
                for part, weight in zip(parts, weights):
                    term = part[i * 2 + g].astype(F32) * two_columns(weight, g, 2 * i)
                    tile = term if tile is None else tile + term
                z_out[zi, cc, g] = tile.astype(BF16)
            z_out[zi, cc, 2] = (stat if i == 0 else pltpu.roll(stat, 128 - 2 * i, 1)).astype(BF16)
        for i in range(count // 2):
            zi, cc = w * pair + i // 2, i % 2

            @pl.when((base + zi != z) | (core != cc))
            def _():
                z_copy(zi, cc).start()

        return carry

    lax.fori_loop(0, 2, back, 0)

    loads[5].wait()
    loads[6].wait()

    @pl.when(is_hub)
    def _():
        z_in[z] = z_out[place, core]

    own = [None, None]
    for g in range(2):
        packed = jnp.zeros((8, 128), F32)
        for r in range(2):
            key = nk_ref[r].astype(F32)[g : g + 1]
            dots = jnp.sum(q_own[r, g * 8 : (g + 1) * 8] * key, axis=1, keepdims=True) * SCALE
            packed = jnp.where(lane == r, dots, packed)
        own[g] = packed
    own = jnp.concatenate(own, axis=0)

    for k in range(nz):
        zz = around(k)

        @pl.when((hub != core) | (zz != z))
        def _():
            there = z_in.at[zz]
            remote(there, there, z_send.at[0, 0], z_recv.at[zz], device(along(1), z, core)).wait_recv()

    parts = [z_in.at[k] for k in range(nz)]
    weights, _ = weights_of([decode(part[2]) for part in parts] + [own])
    tiles = []
    for g in range(2):
        tile = None
        for part, weight in zip(parts, weights):
            term = part[g].astype(F32) * two_columns(weight, g, 0)
            tile = term if tile is None else tile + term
        value = jnp.concatenate(
            [jnp.broadcast_to(nv_ref[r].astype(F32)[g : g + 1], (8, 128)) for r in range(2)], axis=0
        )
        tiles.append(tile + value * two_columns(weights[-1], g, 0))
    for r in range(2):
        out_ref[r] = jnp.concatenate([tiles[g][r * 8 : (r + 1) * 8] for g in range(2)], axis=0).astype(BF16)

    for swap in swaps:
        swap.wait_send()
    for k in range(1, nz):
        qz_copy(k).wait_send()

    @pl.when(hub != core)
    def _():
        qz_copy(0).wait_send()

    for zi in range(half):
        for cc in range(2):

            @pl.when((base + zi != z) | (core != cc))
            def _():
                z_copy(zi, cc).wait_send()

    for k in range(1, ny):
        for w in range(2):
            qy_copy(w, k).wait_send()
            y_copy(w, along(k)).wait_send()


def per_device(ny, nz, queries, cache_keys, cache_values, new_keys, new_values, doc_start, doc_count):
    hbm = pl.BlockSpec(memory_space=pltpu.HBM)
    dma = pltpu.SemaphoreType.DMA
    half = nz // 2
    pair = half // 2
    tiles = 4 * pair + 1
    return pl.pallas_call(
        functools.partial(kernel, ny, nz),
        out_shape=pltpu.VMEM(queries.shape, BF16),
        in_specs=[hbm] * 7,
        out_specs=pl.BlockSpec(memory_space=pltpu.VMEM),
        scratch_shapes=[
            pltpu.VMEM(queries.shape, BF16),
            pltpu.VMEM(new_keys.shape, BF16),
            pltpu.VMEM(new_values.shape, BF16),
            pltpu.SMEM(doc_start.shape[::-1], jnp.int32),
            pltpu.SMEM(doc_count.shape[::-1], jnp.int32),
            pltpu.VMEM((2, 16, 128), BF16),
            pltpu.VMEM((ny, half, 2, 2, 16, 128), BF16),
            pltpu.VMEM((ny, half, 2, 16, 128), BF16),
            pltpu.VMEM((2, 2 * TOK, 128), BF16),
            pltpu.VMEM((2, 2 * TOK, 128), BF16),
            pltpu.VMEM((2, 520, 128), F32),
            pltpu.VMEM((2, 2 * TOK, 256), BF16),
            pltpu.VMEM((2, 2 * TOK, 256), BF16),
            pltpu.VMEM((2, 32 * pair * ny, 2 * TOK), F32),
            pltpu.VMEM((2, ny, tiles, 16, 128), BF16),
            pltpu.VMEM((2, ny, tiles, 16, 128), BF16),
            pltpu.VMEM((half, 2, 3, 16, 128), BF16),
            pltpu.VMEM((nz, 3, 16, 128), BF16),
            dma((7,)),
            dma((2,)), dma((2,)),
            dma((nz,)), dma((half, 2)),
            dma((2, ny - 1)), dma((2, ny - 1)),
            dma((2, ny)), dma((2, ny)),
            dma((half, 2)), dma((nz,)),
        ],
        compiler_params=pltpu.CompilerParams(
            collective_id=0, has_side_effects=True, vmem_limit_bytes=60 * 1024 * 1024
        ),
        name="attention",
    )(
        queries,
        cache_keys.reshape(2 * TOK, 128),
        cache_values.reshape(2 * TOK, 128),
        new_keys,
        new_values,
        doc_start.T,
        doc_count.T,
    )


def solution(mesh):
    ny, nz = 4, mesh.shape["seq"] // 8
    placed = (P("seq", "kvh", None),) * 5 + (P(), P())
    return jax.shard_map(
        functools.partial(per_device, ny, nz),
        mesh=mesh,
        in_specs=placed,
        out_specs=P("seq", "kvh", None),
        check_vma=False,
    )
```

```python
import functools

import jax
import jax.numpy as jnp
from jax import lax
from jax.experimental import pallas as pl
from jax.experimental.pallas import tpu as pltpu
from jax.sharding import PartitionSpec as P

MESH = pl.DeviceIdType.MESH
HD = 128
BLOCK = 512
NBLOCKS = 4
TOK = BLOCK * NBLOCKS
NEG = -1e30
SCALE = HD ** (-0.5)
F32 = jnp.float32
BF16 = jnp.bfloat16


def lanes_of(rows):
    return lax.broadcasted_iota(jnp.int32, (rows, 128), 1)


def encode(stat, count):
    stat = jnp.where(lanes_of(16) < count, stat, 0.0)
    high = stat.astype(BF16).astype(F32)
    rest = stat - high
    middle = rest.astype(BF16).astype(F32)
    low = rest - middle
    return high + pltpu.roll(middle, 32, 1) + pltpu.roll(low, 64, 1)


def decode(tile):
    tile = tile.astype(F32)
    return tile + pltpu.roll(tile, 96, 1) + pltpu.roll(tile, 64, 1)


def weights_of(stats):
    top = functools.reduce(jnp.maximum, stats)
    raw = [jnp.exp(s - top) for s in stats]
    total = functools.reduce(jnp.add, raw)
    inverse = 1.0 / total
    return [w * inverse for w in raw], top + jnp.log(total)


def two_columns(weight, g, column):
    part = weight[g * 8 : (g + 1) * 8]
    return jnp.concatenate(
        [jnp.broadcast_to(part[:, column + r : column + r + 1], (8, 128)) for r in range(2)], axis=0
    )


def by_distance(n, first=1):
    return sorted(range(first, n), key=lambda k: -min(k, n - k))


def kernel(
    ny, nz,
    q_hbm, k_hbm, v_hbm, nk_hbm, nv_hbm, start_hbm, count_hbm, out_ref,
    q_ref, nk_ref, nv_ref, start_ref, count_ref,
    q_mine, qbuf, bias, kraw, vraw, temp, kaug, vaug, scores,
    y_out, y_in, z_out, z_in,
    load_sem, kv_send, kv_recv, qz_send, qz_recv, qy_send, qy_recv,
    y_send, y_recv, z_send, z_recv,
):
    half = nz // 2
    pair = half // 2
    seq = lax.axis_index("seq")
    x = lax.axis_index("kvh")
    core = lax.rem(seq, 2)
    z = lax.rem(lax.div(seq, 2), nz)
    y = lax.div(seq, 2 * nz)
    other = 1 - core
    hub = 1 - lax.div(z, half)
    is_hub = hub == core
    place = lax.rem(z, half)
    base = (1 - core) * half

    def device(yy, zz, cc):
        return ((yy * nz + zz) * 2 + cc, x)

    def along(i):
        return lax.rem(y + i, ny)

    def around(i):
        return lax.rem(z + i, nz)

    def remote(src, dst, send, recv, peer):
        return pltpu.make_async_remote_copy(
            src_ref=src, dst_ref=dst, send_sem=send, recv_sem=recv, device_id=peer, device_id_type=MESH
        )

    loads = [
        pltpu.make_async_copy(src, dst, load_sem.at[i])
        for i, (src, dst) in enumerate(
            [
                (q_hbm, q_ref), (start_hbm, start_ref), (count_hbm, count_ref),
                (k_hbm, kraw.at[0]), (v_hbm, vraw.at[0]), (nk_hbm, nk_ref), (nv_hbm, nv_ref),
            ]
        )
    ]
    loads[0].start()

    barrier = pltpu.get_barrier_semaphore()

    def greet(peer):
        pl.semaphore_signal(barrier, inc=1, device_id=peer, device_id_type=MESH)

    for k in by_distance(nz):
        zz = around(k)
        greet(device(y, zz, hub))

        @pl.when(lax.div(zz, half) == 1 - core)
        def _():
            greet(device(y, zz, 1 - hub))

    for k in by_distance(ny):
        greet(device(along(k), z, core))
    greet(device(y, z, other))
    for load in loads[1:]:
        load.start()

    loads[0].wait()
    q_own = q_ref[...].astype(F32)
    for g in range(2):
        q_mine[g] = jnp.concatenate([q_own[r, g * 8 : (g + 1) * 8] for r in range(2)], axis=0).astype(BF16)

    @pl.when(is_hub)
    def _():
        qbuf[y, place, core] = q_mine[...]

    pl.semaphore_wait(barrier, nz - 1 + half + ny - 1 + jnp.abs(hub - core))

    def qz_copy(k):
        return remote(
            q_mine, qbuf.at[y, place, core], qz_send.at[k], qz_recv.at[place, core], device(y, around(k), hub)
        )

    for k in by_distance(nz):
        qz_copy(k).start()

    @pl.when(hub != core)
    def _():
        qz_copy(0).start()

    swaps = [
        remote(src, dst, kv_send.at[i], kv_recv.at[i], device(y, z, other))
        for i, (src, dst) in enumerate([(k_hbm, kraw.at[1]), (v_hbm, vraw.at[1])])
    ]
    for swap in swaps:
        swap.start()

    lane = lanes_of(8)
    block = jnp.where(lane < NBLOCKS, seq * NBLOCKS + lane, (seq + 1 - 2 * core) * NBLOCKS + lane - NBLOCKS)

    def row_bias(row):
        seen = None
        for i in range(2):
            first = start_ref[i, row]
            inside = (block >= first) & (block < first + count_ref[i, row])
            seen = inside if seen is None else seen | inside
        return jnp.where(seen | (lane >= 2 * NBLOCKS), 0.0, NEG)

    def fill_bias(i, carry):
        yy, zi, cc = lax.div(i, nz), lax.rem(lax.div(i, 2), half), lax.rem(i, 2)
        row = 4 * (yy * nz + base + zi) + 2 * cc
        bias[yy, zi, cc] = jnp.concatenate([row_bias(row), row_bias(row + 1)], axis=0).astype(BF16)
        return carry

    loads[1].wait()
    loads[2].wait()
    lax.fori_loop(0, ny * nz, fill_bias, 0)

    piece = 256

    def split(which):
        def body(i, carry):
            at = pl.multiple_of(which * TOK + i * piece, piece)
            flat = pl.multiple_of(i * 2 * piece, 2 * piece)
            indicator = (lanes_of(piece) == lax.div(at, BLOCK)).astype(F32).astype(BF16)
            temp[0, 0 : 2 * piece] = kraw[which, pl.ds(flat, 2 * piece), :].astype(F32)
            temp[1, 0 : 2 * piece] = vraw[which, pl.ds(flat, 2 * piece), :].astype(F32)
            for g in range(2):
                kaug[g, pl.ds(at, piece), 0:128] = temp[0, pl.ds(g, piece, stride=2), :].astype(BF16)
                kaug[g, pl.ds(at, piece), 128:256] = indicator
                vaug[g, pl.ds(at, piece), 0:128] = temp[1, pl.ds(g, piece, stride=2), :].astype(BF16)
                vaug[g, pl.ds(at, piece), 128:256] = jnp.ones((piece, 128), BF16)
            return carry

        lax.fori_loop(0, TOK // piece, body, 0)

    loads[3].wait()
    loads[4].wait()
    split(0)

    def qy_copy(w, k):
        mine = qbuf.at[y, pl.ds(w * pair, pair)]
        return remote(mine, mine, qy_send.at[w, k - 1], qy_recv.at[w, k - 1], device(along(k), z, core))

    def qy_arrival(w, k):
        there = qbuf.at[along(ny - k), pl.ds(w * pair, pair)]
        return remote(there, there, qy_send.at[w, k - 1], qy_recv.at[w, k - 1], device(along(k), z, core))

    for w in range(2):
        for zi in range(w * pair, (w + 1) * pair):
            for cc in range(2):

                @pl.when((base + zi != z) | (core != cc))
                def _():
                    there = qbuf.at[y, zi, cc]
                    remote(
                        there, there, qz_send.at[0], qz_recv.at[zi, cc], device(along(1), z, core)
                    ).wait_recv()

        for k in by_distance(ny):
            qy_copy(w, k).start()

    for swap in swaps:
        swap.wait_recv()
    split(1)

    rows = 32 * pair
    count = 4 * pair

    def attend(w):
        tops = []
        for g in range(2):
            lhs = jnp.concatenate(
                [
                    qbuf[:, pl.ds(w * pair, pair), :, g].reshape(ny * rows, 128),
                    bias[:, pl.ds(w * pair, pair)].reshape(ny * rows, 128),
                ],
                axis=1,
            )
            top = None
            for b in range(2 * NBLOCKS):
                s = lax.dot_general(
                    lhs, kaug[g, b * BLOCK : (b + 1) * BLOCK, :], (((1,), (1,)), ((), ())),
                    preferred_element_type=F32,
                )
                scores[g, :, b * BLOCK : (b + 1) * BLOCK] = s
                for i in range(BLOCK // 128):
                    part = s[:, i * 128 : (i + 1) * 128]
                    top = part if top is None else jnp.maximum(top, part)
            tops.append(jnp.max(top, axis=1, keepdims=True))
        stats = [[None] * 2 for _ in range(ny)]
        for g in range(2):
            total = None
            for b in range(2 * NBLOCKS):
                s = scores[g, :, b * BLOCK : (b + 1) * BLOCK]
                p = jnp.exp((s - tops[g]) * SCALE).astype(BF16)
                term = jnp.dot(p, vaug[g, b * BLOCK : (b + 1) * BLOCK, :], preferred_element_type=F32)
                total = term if total is None else total + term
            norm = total[:, 128:256]
            out = total[:, 0:128] * (1.0 / norm)
            stat = tops[g] * SCALE + jnp.log(norm)
            for yy in range(ny):
                packed = jnp.zeros((8, 128), F32)
                for k in range(count):
                    at = yy * rows + k * 8
                    packed = jnp.where(lane == k, stat[at : at + 8], packed)
                stats[yy][g] = packed
                for i in range(count // 2):
                    at = yy * rows + i * 16
                    y_out[w, yy, i * 2 + g] = out[at : at + 16].astype(BF16)
        for yy in range(ny):
            y_out[w, yy, count] = encode(jnp.concatenate(stats[yy], axis=0), count).astype(BF16)

    def y_copy(w, yy):
        return remote(
            y_out.at[w, yy], y_in.at[w, y], y_send.at[w, yy], y_recv.at[w, y], device(yy, z, core)
        )

    def forward(w, carry):
        for k in range(1, ny):
            qy_arrival(w, k).wait_recv()
        attend(w)
        for yy in range(ny):

            @pl.when(yy != y)
            def _():
                y_copy(w, yy).start()

        return carry

    lax.fori_loop(0, 2, forward, 0)

    def z_copy(zi, cc):
        return remote(
            z_out.at[zi, cc], z_in.at[z], z_send.at[zi, cc], z_recv.at[z], device(y, base + zi, cc)
        )

    def back(w, carry):
        for k in range(1, ny):
            there = y_in.at[w, along(k)]
            remote(there, there, y_send.at[w, 0], y_recv.at[w, along(k)], device(along(k), z, core)).wait_recv()
        parts = [y_out.at[w, y]] + [y_in.at[w, along(k)] for k in range(1, ny)]
        weights, stat = weights_of([decode(part[count]) for part in parts])
        stat = encode(stat, count)
        for i in (1, 0, 3, 2):
            zi, cc = w * pair + i // 2, i % 2
            z_out[zi, cc, 2] = (stat if i == 0 else pltpu.roll(stat, 128 - 2 * i, 1)).astype(BF16)
            for g in range(2):
                tile = None
                for part, weight in zip(parts, weights):
                    term = part[i * 2 + g].astype(F32) * two_columns(weight, g, 2 * i)
                    tile = term if tile is None else tile + term
                z_out[zi, cc, g] = tile.astype(BF16)

            @pl.when((base + zi != z) | (core != cc))
            def _():
                z_copy(zi, cc).start()

        return carry

    lax.fori_loop(0, 2, back, 0)

    loads[5].wait()
    loads[6].wait()

    @pl.when(is_hub)
    def _():
        z_in[z] = z_out[place, core]

    own = [None, None]
    for g in range(2):
        packed = jnp.zeros((8, 128), F32)
        for r in range(2):
            key = nk_ref[r].astype(F32)[g : g + 1]
            dots = jnp.sum(q_own[r, g * 8 : (g + 1) * 8] * key, axis=1, keepdims=True) * SCALE
            packed = jnp.where(lane == r, dots, packed)
        own[g] = packed
    own = jnp.concatenate(own, axis=0)

    for k in range(nz):
        zz = around(k)

        @pl.when((hub != core) | (zz != z))
        def _():
            there = z_in.at[zz]
            remote(there, there, z_send.at[0, 0], z_recv.at[zz], device(along(1), z, core)).wait_recv()

    parts = [z_in.at[k] for k in range(nz)]
    weights, _ = weights_of([decode(part[2]) for part in parts] + [own])
    tiles = []
    for g in range(2):
        tile = None
        for part, weight in zip(parts, weights):
            term = part[g].astype(F32) * two_columns(weight, g, 0)
            tile = term if tile is None else tile + term
        value = jnp.concatenate(
            [jnp.broadcast_to(nv_ref[r].astype(F32)[g : g + 1], (8, 128)) for r in range(2)], axis=0
        )
        tiles.append(tile + value * two_columns(weights[-1], g, 0))
    for r in range(2):
        out_ref[r] = jnp.concatenate([tiles[g][r * 8 : (r + 1) * 8] for g in range(2)], axis=0).astype(BF16)

    for swap in swaps:
        swap.wait_send()
    for k in range(1, nz):
        qz_copy(k).wait_send()

    @pl.when(hub != core)
    def _():
        qz_copy(0).wait_send()

    for zi in range(half):
        for cc in range(2):

            @pl.when((base + zi != z) | (core != cc))
            def _():
                z_copy(zi, cc).wait_send()

    for k in range(1, ny):
        for w in range(2):
            qy_copy(w, k).wait_send()
            y_copy(w, along(k)).wait_send()


def per_device(ny, nz, queries, cache_keys, cache_values, new_keys, new_values, doc_start, doc_count):
    hbm = pl.BlockSpec(memory_space=pltpu.HBM)
    dma = pltpu.SemaphoreType.DMA
    half = nz // 2
    pair = half // 2
    tiles = 4 * pair + 1
    return pl.pallas_call(
        functools.partial(kernel, ny, nz),
        out_shape=pltpu.VMEM(queries.shape, BF16),
        in_specs=[hbm] * 7,
        out_specs=pl.BlockSpec(memory_space=pltpu.VMEM),
        scratch_shapes=[
            pltpu.VMEM(queries.shape, BF16),
            pltpu.VMEM(new_keys.shape, BF16),
            pltpu.VMEM(new_values.shape, BF16),
            pltpu.SMEM(doc_start.shape[::-1], jnp.int32),
            pltpu.SMEM(doc_count.shape[::-1], jnp.int32),
            pltpu.VMEM((2, 16, 128), BF16),
            pltpu.VMEM((ny, half, 2, 2, 16, 128), BF16),
            pltpu.VMEM((ny, half, 2, 16, 128), BF16),
            pltpu.VMEM((2, 2 * TOK, 128), BF16),
            pltpu.VMEM((2, 2 * TOK, 128), BF16),
            pltpu.VMEM((2, 520, 128), F32),
            pltpu.VMEM((2, 2 * TOK, 256), BF16),
            pltpu.VMEM((2, 2 * TOK, 256), BF16),
            pltpu.VMEM((2, 32 * pair * ny, 2 * TOK), F32),
            pltpu.VMEM((2, ny, tiles, 16, 128), BF16),
            pltpu.VMEM((2, ny, tiles, 16, 128), BF16),
            pltpu.VMEM((half, 2, 3, 16, 128), BF16),
            pltpu.VMEM((nz, 3, 16, 128), BF16),
            dma((7,)),
            dma((2,)), dma((2,)),
            dma((nz,)), dma((half, 2)),
            dma((2, ny - 1)), dma((2, ny - 1)),
            dma((2, ny)), dma((2, ny)),
            dma((half, 2)), dma((nz,)),
        ],
        compiler_params=pltpu.CompilerParams(
            collective_id=0, has_side_effects=True, vmem_limit_bytes=60 * 1024 * 1024
        ),
        name="attention",
    )(
        queries,
        cache_keys.reshape(2 * TOK, 128),
        cache_values.reshape(2 * TOK, 128),
        new_keys,
        new_values,
        doc_start.T,
        doc_count.T,
    )


def solution(mesh):
    ny, nz = 4, mesh.shape["seq"] // 8
    placed = (P("seq", "kvh", None),) * 5 + (P(), P())
    return jax.shard_map(
        functools.partial(per_device, ny, nz),
        mesh=mesh,
        in_specs=placed,
        out_specs=P("seq", "kvh", None),
        check_vma=False,
    )
```
